512 devices in a mesh: shot: 32 (over y_lo, x, core), pair: 16 (over y_hi, z).
Axes of the slice: x: 4, y: 8 (y_hi: 2, y_lo: 4; y = y_hi * 4 + y_lo), z: 8, core: 2. Of those that a mesh axis runs over, the one named last changes fastest.
Arguments:
- spectra: bfloat16 [2, 512, 128, 1024], P(None, 'shot', None, 'pair'), may hold values from -6 to 6
- shot_weight: float32 [512], P('shot'), may hold values from 0.5 to 2
Outputs:
- virtual_gather: bfloat16 [2, 128, 1024, 1024], P(None, 'shot', 'pair')
The draws below stay inside these ranges and needn't reach their ends.
All inputs are finite; a program needn't handle non-finite values.
Results may differ from the reference program's by a relative error of at most 0.0054.
Values may be sent and summed in bfloat16 or wider, within the bound.
No kernel may reach another device: no remote copies, remote signals or barrier semaphores. Data moves between devices by JAX's collectives and lax.ppermute only.
A program may use at most 64 MiB of HBM per device.

```python
import math
import jax
import jax.numpy as jnp
from jax import lax

R = 1024
F = 128
SHOTS = 512


def block_levels(rng, dims, pieces, smallest, high):
    gain, own = 1.0, jax.random.fold_in(rng, 6)
    for axis_at, parts in pieces:
        heights = jnp.exp(jax.random.uniform(jax.random.fold_in(own, axis_at), (parts,), jnp.float32, smallest / len(pieces), high / len(pieces)))
        gain = gain * jnp.repeat(heights, dims[axis_at] // parts).reshape([-1 if axis == axis_at else 1 for axis in range(len(dims))])
    return gain


def gaussian(key, dims, scale, limit, split=(), held_as=jnp.bfloat16):
    entries = jax.random.normal(key, dims, jnp.float32) * scale
    if len(split) > 0:
        entries = block_levels(key, dims, split, -0.22, 0.18) * entries
    return jnp.clip(entries, min=-limit, max=limit).astype(held_as)


def setup_inputs(seed: int = 0) -> dict:
    seeds = jax.random.split(jax.random.key(seed), 3)
    spectra = gaussian(seeds[0], (2, SHOTS, F, R), 1.0, 6.0, ((1, 32), (3, 16)))
    shot_weight = jnp.clip(jnp.exp(math.log(2.0) - 1.3862944 * jax.random.uniform(seeds[1], (SHOTS,), jnp.float32) ** block_levels(seeds[1], (SHOTS,), ((0, 32),), -0.2, 0.2)), 0.5, 2.0)
    return dict(spectra=spectra, shot_weight=shot_weight)


def reference(spectra, shot_weight):
    scaled = (spectra.astype(jnp.float32) * shot_weight[None, :, None, None]).astype(jnp.bfloat16)
    factor = SHOTS ** -0.5
    by_freq = jnp.moveaxis(scaled, 2, 0)

    def frequency_gram(frequency_slab):
        real_part = frequency_slab[0]
        imag_part = frequency_slab[1]
        real_out = jnp.dot(real_part.T, real_part, preferred_element_type=jnp.float32) + jnp.dot(imag_part.T, imag_part, preferred_element_type=jnp.float32)
        imag_out = jnp.dot(real_part.T, imag_part, preferred_element_type=jnp.float32) - jnp.dot(imag_part.T, real_part, preferred_element_type=jnp.float32)
        return (jnp.stack([real_out, imag_out]) * factor).astype(jnp.bfloat16)

    gathers = lax.map(frequency_gram, by_freq)
    return jnp.moveaxis(gathers, 1, 0)
```

```python
import functools

import jax
import jax.numpy as jnp
from jax import lax
from jax.experimental import pallas as pl
from jax.experimental.pallas import tpu as pltpu
from jax.sharding import Mesh, PartitionSpec as P

VMEM = pltpu.MemorySpace.VMEM
SMEM = pltpu.MemorySpace.SMEM
PARAMS = pltpu.CompilerParams(vmem_limit_bytes=32 * 1024 * 1024)


def vmem_call(body, out_shape, in_spaces, scratch=(), flops=0, nbytes=0):
    outs = out_shape if isinstance(out_shape, (list, tuple)) else (out_shape,)
    specs = [pl.BlockSpec(memory_space=VMEM) for _ in outs]
    return pl.pallas_call(
        body,
        out_shape=out_shape,
        in_specs=[pl.BlockSpec(memory_space=s) for s in in_spaces],
        out_specs=specs if isinstance(out_shape, (list, tuple)) else specs[0],
        scratch_shapes=list(scratch),
        compiler_params=PARAMS,
        cost_estimate=pl.CostEstimate(flops=flops, bytes_accessed=nbytes, transcendentals=0),
    )


def scale_kernel(weight_ref, x_ref, out_ref, turned):
    _, shots, chans, bins = x_ref.shape
    planes, depth = turned.shape[0], turned.shape[1]
    for s in range(shots):
        block = x_ref[:, s].reshape(2 * chans, bins).astype(jnp.float32) * weight_ref[s]
        block = block.astype(jnp.bfloat16).astype(jnp.float32)
        turned[:, :, s, :] = block.T.reshape(planes, depth, 2 * chans)
    for z in range(depth):
        out_ref[z] = turned[:, z].astype(jnp.bfloat16)


def split_parts(first, second):
    half = first.shape[1] // 2
    p = jnp.concatenate([first[:, :half], second[:, :half]], axis=1)
    q = jnp.concatenate([first[:, half:], second[:, half:]], axis=1)
    return p, q


def fill_right(right, load, k_rows, factor=None):
    width = right.shape[1] // 2
    for h in range(2):
        base = 2 * h * k_rows
        for j in range(width // 128):
            p, q = load(h, j)
            cols = slice(j * 128, (j + 1) * 128)
            icols = slice(width + j * 128, width + (j + 1) * 128)
            right[base:base + k_rows, cols] = p
            right[base:base + k_rows, icols] = q
            right[base + k_rows:base + 2 * k_rows, cols] = q
            right[base + k_rows:base + 2 * k_rows, icols] = -p


def multiply(left_ref, right, out_ref, factor):
    rows = left_ref.shape[0]
    step = 256
    for r in range(rows // step):
        acc = jnp.dot(
            left_ref[r * step:(r + 1) * step, :], right[...], preferred_element_type=jnp.float32
        )
        out_ref[r * step:(r + 1) * step, :] = (acc * factor).astype(jnp.bfloat16)


def own_kernel(factor, core_ref, a_ref, b_ref, out_ref, left_ref, right):
    depth, k_rows, _ = a_ref.shape
    for h, ref in enumerate((a_ref, b_ref)):
        base = 2 * h * k_rows
        for j in range(depth // 2):
            p, q = split_parts(ref[2 * j], ref[2 * j + 1])
            rows = slice(j * 128, (j + 1) * 128)
            left_ref[rows, base:base + k_rows] = p.T
            left_ref[rows, base + k_rows:base + 2 * k_rows] = q.T
    first = core_ref[0] * (depth // 2)

    def load(h, j):
        ref = (a_ref, b_ref)[h]
        return split_parts(ref[first + 2 * j], ref[first + 2 * j + 1])

    fill_right(right, load, k_rows)
    multiply(left_ref, right, out_ref, factor)


def cross_kernel(factor, core_ref, left_ref, y_ref, out_ref, right):
    _, _, k_rows, _ = y_ref.shape
    core = core_ref[0]

    def load(h, j):
        k_half = core if h == 0 else 1 - core
        return split_parts(y_ref[k_half, 2 * j], y_ref[k_half, 2 * j + 1])

    fill_right(right, load, k_rows)
    multiply(left_ref, right, out_ref, factor)


def assemble_kernel(yh_ref, own_ref, cross_ref, out_ref):
    width = own_ref.shape[3] // 2

    def place(ref, half):
        for part in range(2):
            for quarter in range(2):
                at = (2 * half + quarter) * width
                out_ref[part, :, :, at:at + width] = ref[quarter, :, :, part * width:(part + 1) * width]

    @pl.when(yh_ref[0] == 0)
    def _():
        place(own_ref, 0)
        place(cross_ref, 1)

    @pl.when(yh_ref[0] != 0)
    def _():
        place(own_ref, 1)
        place(cross_ref, 0)


SWAP = [(0, 1), (1, 0)]


def shards(spectra, shot_weight):
    _, shots, bins, chans = spectra.shape
    depth = lax.axis_size("z")
    planes = lax.axis_size("y") * lax.axis_size("x")
    cores = lax.axis_size("c")
    factor = (shots * planes * cores) ** (-0.5)
    core = lax.axis_index("c").astype(jnp.int32).reshape(1)
    yh = lax.axis_index("yh").astype(jnp.int32).reshape(1)
    lanes = 2 * chans
    k_rows = planes * shots
    rows = depth * chans
    width = 2 * (rows // 2)

    turned = jnp.swapaxes(spectra, 2, 3)
    scaled = vmem_call(
        scale_kernel,
        jax.ShapeDtypeStruct((depth, planes, shots, lanes), jnp.bfloat16),
        [SMEM, VMEM],
        [pltpu.VMEM((planes, depth, shots, lanes), jnp.float32)],
        nbytes=2 * spectra.size * 2,
    )(shot_weight, turned)
    scaled = scaled.reshape(bins, shots, lanes)
    mine = lax.all_to_all(scaled, ("z", "y", "x"), 0, 0, tiled=True)
    far = lax.ppermute(mine, "yh", SWAP)
    near = lax.ppermute(mine, "c", SWAP)

    flops = 2 * rows * 4 * k_rows * width
    own, left = vmem_call(
        functools.partial(own_kernel, factor),
        (
            jax.ShapeDtypeStruct((rows, width), jnp.bfloat16),
            jax.ShapeDtypeStruct((rows, 4 * k_rows), jnp.bfloat16),
        ),
        [SMEM, VMEM, VMEM],
        [pltpu.VMEM((4 * k_rows, width), jnp.bfloat16)],
        flops=flops,
        nbytes=4 * rows * width * 2,
    )(core, mine.reshape(depth, k_rows, lanes), near.reshape(depth, k_rows, lanes))
    own = lax.all_to_all(own, "z", 0, 0, tiled=True)
    own = lax.all_to_all(own, "c", 0, 0, tiled=True)

    far = lax.all_to_all(far, "c", 0, 0, tiled=True)
    cross = vmem_call(
        functools.partial(cross_kernel, factor),
        jax.ShapeDtypeStruct((rows, width), jnp.bfloat16),
        [SMEM, VMEM, VMEM],
        [pltpu.VMEM((4 * k_rows, width), jnp.bfloat16)],
        flops=flops,
        nbytes=4 * rows * width * 2,
    )(core, left, far.reshape(cores, depth // 2, k_rows, lanes))
    cross = lax.all_to_all(cross, "z", 0, 0, tiled=True)
    cross = lax.all_to_all(cross, "c", 0, 0, tiled=True)

    per = depth // cores
    shape = (cores, per, chans, width)
    return vmem_call(
        assemble_kernel,
        jax.ShapeDtypeStruct((2, per, chans, 2 * rows), jnp.bfloat16),
        [SMEM, VMEM, VMEM],
        nbytes=4 * rows * width * 2,
    )(yh, own.reshape(shape), cross.reshape(shape))


def solution(mesh):
    fine = Mesh(mesh.devices.reshape(4, 4, 2, 2, 8), ("y", "x", "c", "yh", "z"))
    shot, pair = ("y", "x", "c"), ("yh", "z")
    return jax.shard_map(
        shards,
        mesh=fine,
        in_specs=(P(None, shot, None, pair), P(shot)),
        out_specs=P(None, shot, pair, None),
        check_vma=False,
    )
```

```python
import functools

import jax
import jax.numpy as jnp
from jax import lax
from jax.experimental import pallas as pl
from jax.experimental.pallas import tpu as pltpu
from jax.sharding import Mesh, PartitionSpec as P

VMEM = pltpu.MemorySpace.VMEM
SMEM = pltpu.MemorySpace.SMEM
PARAMS = pltpu.CompilerParams(vmem_limit_bytes=32 * 1024 * 1024)


def vmem_call(body, out_shape, in_spaces, scratch=(), flops=0, nbytes=0):
    outs = out_shape if isinstance(out_shape, (list, tuple)) else (out_shape,)
    specs = [pl.BlockSpec(memory_space=VMEM) for _ in outs]
    return pl.pallas_call(
        body,
        out_shape=out_shape,
        in_specs=[pl.BlockSpec(memory_space=s) for s in in_spaces],
        out_specs=specs if isinstance(out_shape, (list, tuple)) else specs[0],
        scratch_shapes=list(scratch),
        compiler_params=PARAMS,
        cost_estimate=pl.CostEstimate(flops=flops, bytes_accessed=nbytes, transcendentals=0),
    )


def scale_kernel(weight_ref, x_ref, out_ref, turned):
    _, shots, chans, bins = x_ref.shape
    planes, depth = turned.shape[0], turned.shape[1]
    for s in range(shots):
        block = x_ref[:, s].reshape(2 * chans, bins).astype(jnp.float32) * weight_ref[s]
        block = block.astype(jnp.bfloat16).astype(jnp.float32)
        turned[:, :, s, :] = block.T.reshape(planes, depth, 2 * chans)
    for z in range(depth):
        out_ref[z] = turned[:, z].astype(jnp.bfloat16)


def split_parts(first, second):
    half = first.shape[1] // 2
    p = jnp.concatenate([first[:, :half], second[:, :half]], axis=1)
    q = jnp.concatenate([first[:, half:], second[:, half:]], axis=1)
    return p, q


def fill_right(right, load, k_rows, factor=None):
    width = right.shape[1] // 2
    for h in range(2):
        base = 2 * h * k_rows
        for j in range(width // 128):
            p, q = load(h, j)
            cols = slice(j * 128, (j + 1) * 128)
            icols = slice(width + j * 128, width + (j + 1) * 128)
            right[base:base + k_rows, cols] = p
            right[base:base + k_rows, icols] = q
            right[base + k_rows:base + 2 * k_rows, cols] = q
            right[base + k_rows:base + 2 * k_rows, icols] = -p


def multiply(left_ref, right, out_ref, factor):
    rows = left_ref.shape[0]
    step = 256
    for r in range(rows // step):
        acc = jnp.dot(
            left_ref[r * step:(r + 1) * step, :], right[...], preferred_element_type=jnp.float32
        )
        out_ref[r * step:(r + 1) * step, :] = (acc * factor).astype(jnp.bfloat16)


def own_kernel(factor, core_ref, a_ref, b_ref, out_ref, left_ref, right):
    depth, k_rows, _ = a_ref.shape
    for h, ref in enumerate((a_ref, b_ref)):
        base = 2 * h * k_rows
        for j in range(depth // 2):
            p, q = split_parts(ref[2 * j], ref[2 * j + 1])
            rows = slice(j * 128, (j + 1) * 128)
            left_ref[rows, base:base + k_rows] = p.T
            left_ref[rows, base + k_rows:base + 2 * k_rows] = q.T
    first = core_ref[0] * (depth // 2)

    def load(h, j):
        ref = (a_ref, b_ref)[h]
        return split_parts(ref[first + 2 * j], ref[first + 2 * j + 1])

    fill_right(right, load, k_rows)
    multiply(left_ref, right, out_ref, factor)


def cross_kernel(factor, core_ref, left_ref, y_ref, y_other_ref, out_ref, right):
    depth, k_rows, _ = y_ref.shape
    first = core_ref[0] * (depth // 2)

    def load(h, j):
        ref = (y_ref, y_other_ref)[h]
        return split_parts(ref[first + 2 * j], ref[first + 2 * j + 1])

    fill_right(right, load, k_rows)
    multiply(left_ref, right, out_ref, factor)


def assemble_kernel(yh_ref, core_ref, own_ref, own_other_ref, cross_ref, cross_other_ref, out_ref):
    width = own_ref.shape[2] // 2
    bins = own_ref.shape[0] // 2

    def place(ref, core, at):
        mine = slice(core * bins, (core + 1) * bins)
        for part in range(2):
            out_ref[part, :, :, at * width:(at + 1) * width] = ref[mine, :, part * width:(part + 1) * width]

    for yh in range(2):
        for core in range(2):

            @pl.when(jnp.logical_and(yh_ref[0] == yh, core_ref[0] == core))
            def _(yh=yh, core=core):
                place(own_ref, core, 2 * yh + core)
                place(own_other_ref, core, 2 * yh + 1 - core)
                place(cross_ref, core, 2 * (1 - yh) + core)
                place(cross_other_ref, core, 2 * (1 - yh) + 1 - core)


SWAP = [(0, 1), (1, 0)]


def shards(spectra, shot_weight):
    _, shots, bins, chans = spectra.shape
    depth = lax.axis_size("z")
    planes = lax.axis_size("y") * lax.axis_size("x")
    cores = lax.axis_size("c")
    factor = (shots * planes * cores) ** (-0.5)
    core = lax.axis_index("c").astype(jnp.int32).reshape(1)
    yh = lax.axis_index("yh").astype(jnp.int32).reshape(1)
    lanes = 2 * chans
    k_rows = planes * shots
    rows = depth * chans
    width = 2 * (rows // 2)

    turned = jnp.swapaxes(spectra, 2, 3)
    scaled = vmem_call(
        scale_kernel,
        jax.ShapeDtypeStruct((depth, planes, shots, lanes), jnp.bfloat16),
        [SMEM, VMEM],
        [pltpu.VMEM((planes, depth, shots, lanes), jnp.float32)],
        nbytes=2 * spectra.size * 2,
    )(shot_weight, turned)
    scaled = scaled.reshape(bins, shots, lanes)
    mine = lax.all_to_all(scaled, ("z", "y", "x"), 0, 0, tiled=True)
    far = lax.ppermute(mine, "yh", SWAP)
    near = lax.ppermute(mine, "c", SWAP)

    flops = 2 * rows * 4 * k_rows * width
    own, left = vmem_call(
        functools.partial(own_kernel, factor),
        (
            jax.ShapeDtypeStruct((rows, width), jnp.bfloat16),
            jax.ShapeDtypeStruct((rows, 4 * k_rows), jnp.bfloat16),
        ),
        [SMEM, VMEM, VMEM],
        [pltpu.VMEM((4 * k_rows, width), jnp.bfloat16)],
        flops=flops,
        nbytes=4 * rows * width * 2,
    )(core, mine.reshape(depth, k_rows, lanes), near.reshape(depth, k_rows, lanes))
    own = lax.all_to_all(own.reshape(depth, chans, width), "z", 0, 0, tiled=True)

    far_other = lax.ppermute(far, "c", SWAP)
    own, far, far_other = lax.optimization_barrier((own, far, far_other))
    own_other = lax.ppermute(own, "c", SWAP)
    cross = vmem_call(
        functools.partial(cross_kernel, factor),
        jax.ShapeDtypeStruct((rows, width), jnp.bfloat16),
        [SMEM, VMEM, VMEM, VMEM],
        [pltpu.VMEM((4 * k_rows, width), jnp.bfloat16)],
        flops=flops,
        nbytes=4 * rows * width * 2,
    )(core, left, far.reshape(depth, k_rows, lanes), far_other.reshape(depth, k_rows, lanes))
    cross = lax.all_to_all(cross.reshape(depth, chans, width), "z", 0, 0, tiled=True)
    cross_other = lax.ppermute(cross, "c", SWAP)

    return vmem_call(
        assemble_kernel,
        jax.ShapeDtypeStruct((2, depth // cores, chans, 2 * rows), jnp.bfloat16),
        [SMEM, SMEM, VMEM, VMEM, VMEM, VMEM],
        nbytes=4 * rows * width * 2,
    )(yh, core, own, own_other, cross, cross_other)


def solution(mesh):
    fine = Mesh(mesh.devices.reshape(4, 4, 2, 2, 8), ("y", "x", "c", "yh", "z"))
    shot, pair = ("y", "x", "c"), ("yh", "z")
    return jax.shard_map(
        shards,
        mesh=fine,
        in_specs=(P(None, shot, None, pair), P(shot)),
        out_specs=P(None, shot, pair, None),
        check_vma=False,
    )
```

```python
import functools

import jax
import jax.numpy as jnp
from jax import lax
from jax.experimental import pallas as pl
from jax.experimental.pallas import tpu as pltpu
from jax.sharding import Mesh, PartitionSpec as P

VMEM = pltpu.MemorySpace.VMEM
SMEM = pltpu.MemorySpace.SMEM
PARAMS = pltpu.CompilerParams(vmem_limit_bytes=32 * 1024 * 1024)


def vmem_call(body, out_shape, in_spaces, scratch=(), flops=0, nbytes=0):
    outs = out_shape if isinstance(out_shape, (list, tuple)) else (out_shape,)
    specs = [pl.BlockSpec(memory_space=VMEM) for _ in outs]
    return pl.pallas_call(
        body,
        out_shape=out_shape,
        in_specs=[pl.BlockSpec(memory_space=s) for s in in_spaces],
        out_specs=specs if isinstance(out_shape, (list, tuple)) else specs[0],
        scratch_shapes=list(scratch),
        compiler_params=PARAMS,
        cost_estimate=pl.CostEstimate(flops=flops, bytes_accessed=nbytes, transcendentals=0),
    )


def scale_kernel(weight_ref, x_ref, out_ref, turned):
    _, shots, chans, bins = x_ref.shape
    planes, depth = turned.shape[0], turned.shape[1]
    for s in range(shots):
        block = x_ref[:, s].reshape(2 * chans, bins).astype(jnp.float32) * weight_ref[s]
        block = block.astype(jnp.bfloat16).astype(jnp.float32)
        turned[:, :, s, :] = block.T.reshape(planes, depth, 2 * chans)
    for z in range(depth):
        out_ref[z] = turned[:, z].astype(jnp.bfloat16)


def split_parts(first, second):
    half = first.shape[1] // 2
    p = jnp.concatenate([first[:, :half], second[:, :half]], axis=1)
    q = jnp.concatenate([first[:, half:], second[:, half:]], axis=1)
    return p, q


def fill_right(right, load, k_rows, factor=None):
    width = right.shape[1] // 2
    for h in range(2):
        base = 2 * h * k_rows
        for j in range(width // 128):
            p, q = load(h, j)
            cols = slice(j * 128, (j + 1) * 128)
            icols = slice(width + j * 128, width + (j + 1) * 128)
            right[base:base + k_rows, cols] = p
            right[base:base + k_rows, icols] = q
            right[base + k_rows:base + 2 * k_rows, cols] = q
            right[base + k_rows:base + 2 * k_rows, icols] = -p


def multiply(left_ref, right, out_ref, factor):
    rows = left_ref.shape[0]
    step = 256
    for r in range(rows // step):
        acc = jnp.dot(
            left_ref[r * step:(r + 1) * step, :], right[...], preferred_element_type=jnp.float32
        )
        out_ref[r * step:(r + 1) * step, :] = (acc * factor).astype(jnp.bfloat16)


def own_kernel(factor, core_ref, a_ref, b_ref, out_ref, left_ref, right):
    depth, k_rows, _ = a_ref.shape
    for h, ref in enumerate((a_ref, b_ref)):
        base = 2 * h * k_rows
        for j in range(depth // 2):
            p, q = split_parts(ref[2 * j], ref[2 * j + 1])
            rows = slice(j * 128, (j + 1) * 128)
            left_ref[rows, base:base + k_rows] = p.T
            left_ref[rows, base + k_rows:base + 2 * k_rows] = q.T
    first = core_ref[0] * (depth // 2)

    def load(h, j):
        ref = (a_ref, b_ref)[h]
        return split_parts(ref[first + 2 * j], ref[first + 2 * j + 1])

    fill_right(right, load, k_rows)
    multiply(left_ref, right, out_ref, factor)


def right_kernel(y_ref, y_other_ref, right):
    k_rows = y_ref.shape[1]

    def load(h, j):
        ref = (y_ref, y_other_ref)[h]
        return split_parts(ref[2 * j], ref[2 * j + 1])

    fill_right(right, load, k_rows)


def cross_kernel(factor, left_ref, right, out_ref):
    multiply(left_ref, right, out_ref, factor)


def assemble_kernel(yh_ref, core_ref, own_ref, own_other_ref, cross_ref, cross_other_ref, out_ref):
    width = own_ref.shape[2] // 2
    bins = own_ref.shape[0] // 2

    def place(ref, core, at):
        mine = slice(core * bins, (core + 1) * bins)
        for part in range(2):
            out_ref[part, :, :, at * width:(at + 1) * width] = ref[mine, :, part * width:(part + 1) * width]

    for yh in range(2):
        for core in range(2):

            @pl.when(jnp.logical_and(yh_ref[0] == yh, core_ref[0] == core))
            def _(yh=yh, core=core):
                place(own_ref, core, 2 * yh + core)
                place(own_other_ref, core, 2 * yh + 1 - core)
                place(cross_ref, core, 2 * (1 - yh) + core)
                place(cross_other_ref, core, 2 * (1 - yh) + 1 - core)


SWAP = [(0, 1), (1, 0)]


def shards(spectra, shot_weight):
    _, shots, bins, chans = spectra.shape
    depth = lax.axis_size("z")
    planes = lax.axis_size("y") * lax.axis_size("x")
    cores = lax.axis_size("c")
    factor = (shots * planes * cores) ** (-0.5)
    core = lax.axis_index("c").astype(jnp.int32).reshape(1)
    yh = lax.axis_index("yh").astype(jnp.int32).reshape(1)
    lanes = 2 * chans
    k_rows = planes * shots
    rows = depth * chans
    width = 2 * (rows // 2)

    turned = jnp.swapaxes(spectra, 2, 3)
    scaled = vmem_call(
        scale_kernel,
        jax.ShapeDtypeStruct((depth, planes, shots, lanes), jnp.bfloat16),
        [SMEM, VMEM],
        [pltpu.VMEM((planes, depth, shots, lanes), jnp.float32)],
        nbytes=2 * spectra.size * 2,
    )(shot_weight, turned)
    scaled = scaled.reshape(bins, shots, lanes)
    mine = lax.all_to_all(scaled, ("z", "y", "x"), 0, 0, tiled=True)
    half = bins // cores
    first = lax.axis_index("c") * half
    far = lax.ppermute(lax.dynamic_slice_in_dim(mine, first, half), "yh", SWAP)
    near = lax.ppermute(mine, "c", SWAP)
    far_other = lax.ppermute(lax.dynamic_slice_in_dim(near, first, half), "yh", SWAP)

    flops = 2 * rows * 4 * k_rows * width
    own, left = vmem_call(
        functools.partial(own_kernel, factor),
        (
            jax.ShapeDtypeStruct((rows, width), jnp.bfloat16),
            jax.ShapeDtypeStruct((rows, 4 * k_rows), jnp.bfloat16),
        ),
        [SMEM, VMEM, VMEM],
        [pltpu.VMEM((4 * k_rows, width), jnp.bfloat16)],
        flops=flops,
        nbytes=4 * rows * width * 2,
    )(core, mine.reshape(depth, k_rows, lanes), near.reshape(depth, k_rows, lanes))
    own = lax.all_to_all(own.reshape(depth, chans, width), "z", 0, 0, tiled=True)
    right = vmem_call(
        right_kernel,
        jax.ShapeDtypeStruct((4 * k_rows, width), jnp.bfloat16),
        [VMEM, VMEM],
        flops=40 * flops,
    )(
        far.reshape(depth // cores, k_rows, lanes),
        far_other.reshape(depth // cores, k_rows, lanes),
    )
    own, right = lax.optimization_barrier((own, right))
    own_other = lax.ppermute(own, "c", SWAP)
    cross = vmem_call(
        functools.partial(cross_kernel, factor),
        jax.ShapeDtypeStruct((rows, width), jnp.bfloat16),
        [VMEM, VMEM],
        flops=flops,
        nbytes=4 * rows * width * 2,
    )(left, right)
    cross = lax.all_to_all(cross.reshape(depth, chans, width), "z", 0, 0, tiled=True)
    cross_other = lax.ppermute(cross, "c", SWAP)

    return vmem_call(
        assemble_kernel,
        jax.ShapeDtypeStruct((2, depth // cores, chans, 2 * rows), jnp.bfloat16),
        [SMEM, SMEM, VMEM, VMEM, VMEM, VMEM],
        nbytes=4 * rows * width * 2,
    )(yh, core, own, own_other, cross, cross_other)


def solution(mesh):
    fine = Mesh(mesh.devices.reshape(4, 4, 2, 2, 8), ("y", "x", "c", "yh", "z"))
    shot, pair = ("y", "x", "c"), ("yh", "z")
    return jax.shard_map(
        shards,
        mesh=fine,
        in_specs=(P(None, shot, None, pair), P(shot)),
        out_specs=P(None, shot, pair, None),
        check_vma=False,
    )
```

```python
import functools

import jax
import jax.numpy as jnp
from jax import lax
from jax.experimental import pallas as pl
from jax.experimental.pallas import tpu as pltpu
from jax.sharding import Mesh, PartitionSpec as P

VMEM = pltpu.MemorySpace.VMEM
SMEM = pltpu.MemorySpace.SMEM
HBM = pltpu.MemorySpace.HBM
STEPS = 4
PARAMS = pltpu.CompilerParams(vmem_limit_bytes=32 * 1024 * 1024)


def vmem_call(body, out_shape, in_spaces, scratch=(), flops=0, nbytes=0, params=PARAMS):
    outs = out_shape if isinstance(out_shape, (list, tuple)) else (out_shape,)
    specs = [pl.BlockSpec(memory_space=VMEM) for _ in outs]
    return pl.pallas_call(
        body,
        out_shape=out_shape,
        in_specs=[pl.BlockSpec(memory_space=s) for s in in_spaces],
        out_specs=specs if isinstance(out_shape, (list, tuple)) else specs[0],
        scratch_shapes=list(scratch),
        compiler_params=params,
        cost_estimate=pl.CostEstimate(flops=flops, bytes_accessed=nbytes, transcendentals=0),
    )


def scale_kernel(weight_hbm, x_hbm, out_ref, weight_ref, x_ref, turned, sems):
    _, shots, chans, bins = x_ref.shape
    planes, depth = turned.shape[0], turned.shape[1]
    step = shots // STEPS
    weight_copy = pltpu.make_async_copy(weight_hbm, weight_ref, sems.at[STEPS])
    weight_copy.start()
    copies = []
    for i in range(STEPS):
        some = pl.ds(i * step, step)
        copies.append(pltpu.make_async_copy(x_hbm.at[:, some], x_ref.at[:, some], sems.at[i]))
        copies[-1].start()
    weight_copy.wait()
    for s in range(shots):
        if s % step == 0:
            copies[s // step].wait()
        block = x_ref[:, s].reshape(2 * chans, bins).astype(jnp.float32) * weight_ref[s]
        block = block.astype(jnp.bfloat16).astype(jnp.float32)
        turned[:, :, s, :] = block.T.reshape(planes, depth, 2 * chans)
    for z in range(depth):
        out_ref[z] = turned[:, z].astype(jnp.bfloat16)


def split_parts(first, second):
    half = first.shape[1] // 2
    p = jnp.concatenate([first[:, :half], second[:, :half]], axis=1)
    q = jnp.concatenate([first[:, half:], second[:, half:]], axis=1)
    return p, q


def fill_right(right, base, load, k_rows):
    width = right.shape[1] // 2
    for j in range(width // 128):
        p, q = load(j)
        cols = slice(j * 128, (j + 1) * 128)
        icols = slice(width + j * 128, width + (j + 1) * 128)
        right[base:base + k_rows, cols] = p
        right[base:base + k_rows, icols] = q
        right[base + k_rows:base + 2 * k_rows, cols] = q
        right[base + k_rows:base + 2 * k_rows, icols] = -p


def multiply(left_ref, rights, out_ref, factor):
    rows = left_ref.shape[0]
    step = 256
    for r in range(rows // step):
        at, acc = 0, None
        for right in rights:
            depth = right.shape[0]
            term = jnp.dot(
                left_ref[r * step:(r + 1) * step, at:at + depth],
                right[...],
                preferred_element_type=jnp.float32,
            )
            acc = term if acc is None else acc + term
            at += depth
        out_ref[r * step:(r + 1) * step, :] = (acc * factor).astype(jnp.bfloat16)


def own_kernel(factor, core_ref, a_ref, b_ref, out_ref, left_ref, right):
    depth, k_rows, _ = a_ref.shape
    for h, ref in enumerate((a_ref, b_ref)):
        base = 2 * h * k_rows
        for j in range(depth // 2):
            p, q = split_parts(ref[2 * j], ref[2 * j + 1])
            rows = slice(j * 128, (j + 1) * 128)
            left_ref[rows, base:base + k_rows] = p.T
            left_ref[rows, base + k_rows:base + 2 * k_rows] = q.T
    first = core_ref[0] * (depth // 2)

    for h, ref in enumerate((a_ref, b_ref)):

        def load(j, ref=ref):
            return split_parts(ref[first + 2 * j], ref[first + 2 * j + 1])

        fill_right(right, 2 * h * k_rows, load, k_rows)
    multiply(left_ref, (right,), out_ref, factor)


def right_kernel(y_ref, right):
    fill_right(right, 0, lambda j: split_parts(y_ref[2 * j], y_ref[2 * j + 1]), y_ref.shape[1])


def cross_kernel(factor, left_ref, right_ref, right_other_ref, out_ref):
    multiply(left_ref, (right_ref, right_other_ref), out_ref, factor)


def place_kernel(pieces, half, yh_ref, core_ref, *refs):
    sources, out_hbm, sems = refs[:len(pieces)], refs[-2], refs[-1]
    core = core_ref[0]
    bins, width = out_hbm.shape[1], out_hbm.shape[3] // 4
    copies = []
    for n, (piece, source) in enumerate(zip(pieces, sources)):
        bins_at = core * bins if piece == 0 else 0
        column = (2 * ((yh_ref[0] + half) % 2) + (core + piece) % 2) * width
        for part in range(2):
            copies.append(
                pltpu.make_async_copy(
                    source.at[pl.ds(bins_at, bins), :, pl.ds(part * width, width)],
                    out_hbm.at[part, :, :, pl.ds(pl.multiple_of(column, width), width)],
                    sems.at[2 * n + part],
                )
            )
            copies[-1].start()
    for copy in copies:
        copy.wait()


def place(pieces, half, yh, core, sources, shape, out=None):
    extra = [] if out is None else [out]
    return pl.pallas_call(
        functools.partial(place_kernel, pieces, half),
        out_shape=jax.ShapeDtypeStruct(shape, jnp.bfloat16),
        in_specs=[pl.BlockSpec(memory_space=SMEM)] * 2
        + [pl.BlockSpec(memory_space=VMEM)] * len(sources)
        + [pl.BlockSpec(memory_space=HBM)] * len(extra),
        out_specs=pl.BlockSpec(memory_space=HBM),
        scratch_shapes=[pltpu.SemaphoreType.DMA((2 * len(sources),))],
        input_output_aliases={2 + len(sources): 0} if extra else {},
        compiler_params=PARAMS,
        cost_estimate=pl.CostEstimate(flops=0, bytes_accessed=2 ** 20, transcendentals=0),
    )(yh, core, *sources, *extra)


SWAP = [(0, 1), (1, 0)]


def shards(spectra, shot_weight):
    _, shots, bins, chans = spectra.shape
    depth = lax.axis_size("z")
    planes = lax.axis_size("y") * lax.axis_size("x")
    cores = lax.axis_size("c")
    factor = (shots * planes * cores) ** (-0.5)
    core = lax.axis_index("c").astype(jnp.int32).reshape(1)
    yh = lax.axis_index("yh").astype(jnp.int32).reshape(1)
    lanes = 2 * chans
    k_rows = planes * shots
    rows = depth * chans
    width = 2 * (rows // 2)

    turned = jnp.swapaxes(spectra, 2, 3)
    scaled = vmem_call(
        scale_kernel,
        jax.ShapeDtypeStruct((depth, planes, shots, lanes), jnp.bfloat16),
        [HBM, HBM],
        [
            pltpu.SMEM((shots,), jnp.float32),
            pltpu.VMEM((2, shots, chans, bins), jnp.bfloat16),
            pltpu.VMEM((planes, depth, shots, lanes), jnp.float32),
            pltpu.SemaphoreType.DMA((STEPS + 1,)),
        ],
        nbytes=2 * spectra.size * 2,
        params=pltpu.CompilerParams(vmem_limit_bytes=56 * 1024 * 1024),
    )(shot_weight, turned)
    scaled = scaled.reshape(bins, shots, lanes)
    mine = lax.all_to_all(scaled, ("z", "y", "x"), 0, 0, tiled=True)
    half = bins // cores
    first = lax.axis_index("c") * half
    far = lax.ppermute(lax.dynamic_slice_in_dim(mine, first, half), "yh", SWAP)
    near = lax.ppermute(mine, "c", SWAP)

    flops = 2 * rows * 4 * k_rows * width
    own, left = vmem_call(
        functools.partial(own_kernel, factor),
        (
            jax.ShapeDtypeStruct((rows, width), jnp.bfloat16),
            jax.ShapeDtypeStruct((rows, 4 * k_rows), jnp.bfloat16),
        ),
        [SMEM, VMEM, VMEM],
        [pltpu.VMEM((4 * k_rows, width), jnp.bfloat16)],
        flops=flops,
        nbytes=4 * rows * width * 2,
    )(core, mine.reshape(depth, k_rows, lanes), near.reshape(depth, k_rows, lanes))
    own, near = lax.optimization_barrier((own, near))
    far_other = lax.ppermute(lax.dynamic_slice_in_dim(near, first, half), "yh", SWAP)
    own = lax.all_to_all(own.reshape(depth, chans, width), "z", 0, 0, tiled=True)
    def right_of(part, weight):
        return vmem_call(
            right_kernel,
            jax.ShapeDtypeStruct((2 * k_rows, width), jnp.bfloat16),
            [VMEM],
            flops=weight * flops,
        )(part.reshape(depth // cores, k_rows, lanes))

    right, right_other = right_of(far, 15), right_of(far_other, 0)
    own, right, right_other = lax.optimization_barrier((own, right, right_other))
    per = depth // cores
    shape = (2, per, chans, 2 * rows)
    theirs = (1 - lax.axis_index("c")) * per
    own_other = lax.ppermute(lax.dynamic_slice_in_dim(own, theirs, per), "c", SWAP)
    cross = vmem_call(
        functools.partial(cross_kernel, factor),
        jax.ShapeDtypeStruct((rows, width), jnp.bfloat16),
        [VMEM, VMEM, VMEM],
        flops=flops,
        nbytes=4 * rows * width * 2,
    )(left, right, right_other)
    cross = lax.all_to_all(cross.reshape(depth, chans, width), "z", 0, 0, tiled=True)
    out = place((0, 1), 0, yh, core, (own, own_other), shape)
    out, cross = lax.optimization_barrier((out, cross))
    cross_other = lax.ppermute(lax.dynamic_slice_in_dim(cross, theirs, per), "c", SWAP)
    out = place((0,), 1, yh, core, (cross,), shape, out)
    return place((1,), 1, yh, core, (cross_other,), shape, out)


def solution(mesh):
    fine = Mesh(mesh.devices.reshape(4, 4, 2, 2, 8), ("y", "x", "c", "yh", "z"))
    shot, pair = ("y", "x", "c"), ("yh", "z")
    return jax.shard_map(
        shards,
        mesh=fine,
        in_specs=(P(None, shot, None, pair), P(shot)),
        out_specs=P(None, shot, pair, None),
        check_vma=False,
    )
```

```python
import functools

import jax
import jax.numpy as jnp
from jax import lax
from jax.experimental import pallas as pl
from jax.experimental.pallas import tpu as pltpu
from jax.sharding import Mesh, PartitionSpec as P

VMEM = pltpu.MemorySpace.VMEM
SMEM = pltpu.MemorySpace.SMEM
HBM = pltpu.MemorySpace.HBM
STEPS = 4
PARAMS = pltpu.CompilerParams(vmem_limit_bytes=32 * 1024 * 1024)


def vmem_call(body, out_shape, in_spaces, scratch=(), flops=0, nbytes=0, params=PARAMS):
    outs = out_shape if isinstance(out_shape, (list, tuple)) else (out_shape,)
    specs = [pl.BlockSpec(memory_space=VMEM) for _ in outs]
    return pl.pallas_call(
        body,
        out_shape=out_shape,
        in_specs=[pl.BlockSpec(memory_space=s) for s in in_spaces],
        out_specs=specs if isinstance(out_shape, (list, tuple)) else specs[0],
        scratch_shapes=list(scratch),
        compiler_params=params,
        cost_estimate=pl.CostEstimate(flops=flops, bytes_accessed=nbytes, transcendentals=0),
    )


def scale_kernel(weight_hbm, x_hbm, out_ref, weight_ref, x_ref, turned, sems):
    _, shots, chans, bins = x_ref.shape
    planes, depth = turned.shape[0], turned.shape[1]
    step = shots // STEPS
    weight_copy = pltpu.make_async_copy(weight_hbm, weight_ref, sems.at[STEPS])
    weight_copy.start()
    copies = []
    for i in range(STEPS):
        some = pl.ds(i * step, step)
        copies.append(pltpu.make_async_copy(x_hbm.at[:, some], x_ref.at[:, some], sems.at[i]))
        copies[-1].start()
    weight_copy.wait()
    for s in range(shots):
        if s % step == 0:
            copies[s // step].wait()
        block = x_ref[:, s].reshape(2 * chans, bins).astype(jnp.float32) * weight_ref[s]
        block = block.astype(jnp.bfloat16).astype(jnp.float32)
        turned[:, :, s, :] = block.T.reshape(planes, depth, 2 * chans)
    for z in range(depth):
        out_ref[z] = turned[:, z].astype(jnp.bfloat16)


def split_parts(first, second):
    half = first.shape[1] // 2
    p = jnp.concatenate([first[:, :half], second[:, :half]], axis=1)
    q = jnp.concatenate([first[:, half:], second[:, half:]], axis=1)
    return p, q


def fill_right(right, base, load, k_rows):
    width = right.shape[1] // 2
    for j in range(width // 128):
        p, q = load(j)
        cols = slice(j * 128, (j + 1) * 128)
        icols = slice(width + j * 128, width + (j + 1) * 128)
        right[base:base + k_rows, cols] = p
        right[base:base + k_rows, icols] = q
        right[base + k_rows:base + 2 * k_rows, cols] = q
        right[base + k_rows:base + 2 * k_rows, icols] = -p


def multiply(left_ref, rights, out_ref, factor):
    rows = left_ref.shape[0]
    step = 256
    for r in range(rows // step):
        at, acc = 0, None
        for right in rights:
            depth = right.shape[0]
            term = jnp.dot(
                left_ref[r * step:(r + 1) * step, at:at + depth],
                right[...],
                preferred_element_type=jnp.float32,
            )
            acc = term if acc is None else acc + term
            at += depth
        out_ref[r * step:(r + 1) * step, :] = (acc * factor).astype(jnp.bfloat16)


def left_kernel(a_ref, b_ref, left_ref):
    blocks, k_rows, _ = a_ref.shape
    for h, ref in enumerate((a_ref, b_ref)):
        base = 2 * h * k_rows
        for j in range(blocks // 2):
            p, q = split_parts(ref[2 * j], ref[2 * j + 1])
            rows = slice(j * 128, (j + 1) * 128)
            left_ref[rows, base:base + k_rows] = p.T
            left_ref[rows, base + k_rows:base + 2 * k_rows] = q.T


def gram_kernel(factor, zl_ref, left_ref, a_ref, b_ref, a_far_ref, b_far_ref, out_ref, right):
    k_rows = a_ref.shape[1]
    for zl in range(2):

        @pl.when(zl_ref[0] == zl)
        def _(zl=zl):
            for h, pair in enumerate(((a_ref, a_far_ref), (b_ref, b_far_ref))):

                def load(j, pair=pair):
                    return split_parts(pair[zl][j], pair[1 - zl][j])

                fill_right(right, 2 * h * k_rows, load, k_rows)

    multiply(left_ref, (right,), out_ref, factor)


def place_kernel(piece, core_ref, source, *refs):
    out_hbm, sems = refs[-2], refs[-1]
    core = core_ref[0]
    bins, width = out_hbm.shape[1], out_hbm.shape[3] // 2
    bins_at = core * bins if piece == 0 else 0
    column = pl.multiple_of((core + piece) % 2 * width, width)
    copies = []
    for part in range(2):
        copies.append(
            pltpu.make_async_copy(
                source.at[pl.ds(bins_at, bins), :, pl.ds(part * width, width)],
                out_hbm.at[part, :, :, pl.ds(column, width)],
                sems.at[part],
            )
        )
        copies[-1].start()
    for copy in copies:
        copy.wait()


def place(piece, core, source, shape, out=None):
    extra = [] if out is None else [out]
    return pl.pallas_call(
        functools.partial(place_kernel, piece),
        out_shape=jax.ShapeDtypeStruct(shape, jnp.bfloat16),
        in_specs=[pl.BlockSpec(memory_space=SMEM), pl.BlockSpec(memory_space=VMEM)]
        + [pl.BlockSpec(memory_space=HBM)] * len(extra),
        out_specs=pl.BlockSpec(memory_space=HBM),
        scratch_shapes=[pltpu.SemaphoreType.DMA((2,))],
        input_output_aliases={2: 0} if extra else {},
        compiler_params=PARAMS,
        cost_estimate=pl.CostEstimate(flops=0, bytes_accessed=2 ** 20, transcendentals=0),
    )(core, source, *extra)


SWAP = [(0, 1), (1, 0)]


def shards(spectra, shot_weight):
    _, shots, bins, chans = spectra.shape
    depth = lax.axis_size("yh") * lax.axis_size("zh")
    planes = lax.axis_size("y") * lax.axis_size("x")
    cores = lax.axis_size("c")
    factor = (shots * planes * cores) ** (-0.5)
    core = lax.axis_index("c").astype(jnp.int32).reshape(1)
    zl = lax.axis_index("zl").astype(jnp.int32).reshape(1)
    lanes = 2 * chans
    k_rows = planes * shots
    rows = depth * chans
    width = 2 * rows

    turned = jnp.swapaxes(spectra, 2, 3)
    scaled = vmem_call(
        scale_kernel,
        jax.ShapeDtypeStruct((depth, planes, shots, lanes), jnp.bfloat16),
        [HBM, HBM],
        [
            pltpu.SMEM((shots,), jnp.float32),
            pltpu.VMEM((2, shots, chans, bins), jnp.bfloat16),
            pltpu.VMEM((planes, depth, shots, lanes), jnp.float32),
            pltpu.SemaphoreType.DMA((STEPS + 1,)),
        ],
        nbytes=2 * spectra.size * 2,
        params=pltpu.CompilerParams(vmem_limit_bytes=56 * 1024 * 1024),
    )(shot_weight, turned)
    scaled = scaled.reshape(bins, shots, lanes)
    mine = lax.all_to_all(scaled, ("yh", "zh", "y", "x"), 0, 0, tiled=True)
    half = bins // cores
    first = lax.axis_index("c") * half
    near = lax.ppermute(mine, "c", SWAP)
    mine_part = lax.dynamic_slice_in_dim(mine, first, half)
    near_part = lax.dynamic_slice_in_dim(near, first, half)
    far = lax.ppermute(mine_part, "zl", SWAP)
    far_other = lax.ppermute(near_part, "zl", SWAP)

    left = vmem_call(
        left_kernel,
        jax.ShapeDtypeStruct((rows, 4 * k_rows), jnp.bfloat16),
        [VMEM, VMEM],
        nbytes=4 * rows * width,
    )(mine.reshape(depth, k_rows, lanes), near.reshape(depth, k_rows, lanes))
    parts = [x.reshape(depth // cores, k_rows, lanes) for x in (mine_part, near_part, far, far_other)]
    gram = vmem_call(
        functools.partial(gram_kernel, factor),
        jax.ShapeDtypeStruct((rows, width), jnp.bfloat16),
        [SMEM] + [VMEM] * 5,
        [pltpu.VMEM((4 * k_rows, width), jnp.bfloat16)],
        flops=2 * rows * 4 * k_rows * width,
        nbytes=4 * rows * width * 2,
    )(zl, left, *parts)
    gram = lax.all_to_all(gram.reshape(depth, chans, width), ("yh", "zh"), 0, 0, tiled=True)
    per = depth // cores
    theirs = (1 - lax.axis_index("c")) * per
    other = lax.ppermute(lax.dynamic_slice_in_dim(gram, theirs, per), "c", SWAP)
    shape = (2, per, chans, 2 * rows)
    return place(1, core, other, shape, place(0, core, gram, shape))


def solution(mesh):
    fine = Mesh(mesh.devices.reshape(4, 4, 2, 2, 4, 2), ("y", "x", "c", "yh", "zh", "zl"))
    shot, pair = ("y", "x", "c"), ("yh", "zh", "zl")
    return jax.shard_map(
        shards,
        mesh=fine,
        in_specs=(P(None, shot, None, pair), P(shot)),
        out_specs=P(None, shot, pair, None),
        check_vma=False,
    )
```

```python
import functools

import jax
import jax.numpy as jnp
from jax import lax
from jax.experimental import pallas as pl
from jax.experimental.pallas import tpu as pltpu
from jax.sharding import Mesh, PartitionSpec as P

VMEM = pltpu.MemorySpace.VMEM
SMEM = pltpu.MemorySpace.SMEM
HBM = pltpu.MemorySpace.HBM
STEPS = 4
PARAMS = pltpu.CompilerParams(vmem_limit_bytes=32 * 1024 * 1024)


def vmem_call(body, out_shape, in_spaces, scratch=(), flops=0, nbytes=0, params=PARAMS):
    outs = out_shape if isinstance(out_shape, (list, tuple)) else (out_shape,)
    specs = [pl.BlockSpec(memory_space=VMEM) for _ in outs]
    return pl.pallas_call(
        body,
        out_shape=out_shape,
        in_specs=[pl.BlockSpec(memory_space=s) for s in in_spaces],
        out_specs=specs if isinstance(out_shape, (list, tuple)) else specs[0],
        scratch_shapes=list(scratch),
        compiler_params=params,
        cost_estimate=pl.CostEstimate(flops=flops, bytes_accessed=nbytes, transcendentals=0),
    )


def scale_kernel(weight_hbm, x_hbm, out_ref, weight_ref, x_ref, turned, sems):
    _, shots, chans, bins = x_ref.shape
    planes, depth = turned.shape[0], turned.shape[1]
    step = shots // STEPS
    weight_copy = pltpu.make_async_copy(weight_hbm, weight_ref, sems.at[STEPS])
    weight_copy.start()
    copies = []
    for i in range(STEPS):
        some = pl.ds(i * step, step)
        copies.append(pltpu.make_async_copy(x_hbm.at[:, some], x_ref.at[:, some], sems.at[i]))
        copies[-1].start()
    weight_copy.wait()
    for s in range(shots):
        if s % step == 0:
            copies[s // step].wait()
        block = x_ref[:, s].reshape(2 * chans, bins).astype(jnp.float32) * weight_ref[s]
        block = block.astype(jnp.bfloat16).astype(jnp.float32)
        turned[:, :, s, :] = block.T.reshape(planes, depth, 2 * chans)
    for z in range(depth):
        out_ref[z] = turned[:, z].astype(jnp.bfloat16)


def split_parts(first, second):
    half = first.shape[1] // 2
    p = jnp.concatenate([first[:, :half], second[:, :half]], axis=1)
    q = jnp.concatenate([first[:, half:], second[:, half:]], axis=1)
    return p, q


def fill_right(right, base, load, k_rows):
    width = right.shape[1] // 2
    for j in range(width // 128):
        p, q = load(j)
        cols = slice(j * 128, (j + 1) * 128)
        icols = slice(width + j * 128, width + (j + 1) * 128)
        right[base:base + k_rows, cols] = p
        right[base:base + k_rows, icols] = q
        right[base + k_rows:base + 2 * k_rows, cols] = q
        right[base + k_rows:base + 2 * k_rows, icols] = -p


def multiply(left_ref, rights, out_ref, factor):
    rows = left_ref.shape[0]
    step = 256
    for r in range(rows // step):
        at, acc = 0, None
        for right in rights:
            depth = right.shape[0]
            term = jnp.dot(
                left_ref[r * step:(r + 1) * step, at:at + depth],
                right[...],
                preferred_element_type=jnp.float32,
            )
            acc = term if acc is None else acc + term
            at += depth
        out_ref[r * step:(r + 1) * step, :] = (acc * factor).astype(jnp.bfloat16)


def own_kernel(factor, core_ref, a_ref, b_ref, out_ref, left_ref, right):
    depth, k_rows, _ = a_ref.shape
    for h, ref in enumerate((a_ref, b_ref)):
        base = 2 * h * k_rows
        for j in range(depth // 2):
            p, q = split_parts(ref[2 * j], ref[2 * j + 1])
            rows = slice(j * 128, (j + 1) * 128)
            left_ref[rows, base:base + k_rows] = p.T
            left_ref[rows, base + k_rows:base + 2 * k_rows] = q.T
    first = core_ref[0] * (depth // 2)

    for h, ref in enumerate((a_ref, b_ref)):

        def load(j, ref=ref):
            return split_parts(ref[first + 2 * j], ref[first + 2 * j + 1])

        fill_right(right, 2 * h * k_rows, load, k_rows)
    multiply(left_ref, (right,), out_ref, factor)


def first_kernel(left_ref, y_ref, out_ref, right):
    k_rows = y_ref.shape[1]
    fill_right(right, 0, lambda j: split_parts(y_ref[2 * j], y_ref[2 * j + 1]), k_rows)
    out_ref[...] = jnp.dot(
        left_ref[:, :2 * k_rows], right[...], preferred_element_type=jnp.float32
    )


def second_kernel(factor, left_ref, y_ref, first_ref, out_ref, right):
    k_rows, step = y_ref.shape[1], 128
    fill_right(right, 0, lambda j: split_parts(y_ref[2 * j], y_ref[2 * j + 1]), k_rows)
    for r in range(left_ref.shape[0] // step):
        rows = slice(r * step, (r + 1) * step)
        acc = first_ref[rows] + jnp.dot(
            left_ref[rows, 2 * k_rows:], right[...], preferred_element_type=jnp.float32
        )
        out_ref[rows] = (acc * factor).astype(jnp.bfloat16)


def place_kernel(pieces, half, yh_ref, core_ref, *refs):
    sources, out_hbm, sems = refs[:len(pieces)], refs[-2], refs[-1]
    core = core_ref[0]
    bins, width = out_hbm.shape[1], out_hbm.shape[3] // 4
    copies = []
    for n, (piece, source) in enumerate(zip(pieces, sources)):
        bins_at = core * bins if piece == 0 else 0
        column = (2 * ((yh_ref[0] + half) % 2) + (core + piece) % 2) * width
        for part in range(2):
            copies.append(
                pltpu.make_async_copy(
                    source.at[pl.ds(bins_at, bins), :, pl.ds(part * width, width)],
                    out_hbm.at[part, :, :, pl.ds(pl.multiple_of(column, width), width)],
                    sems.at[2 * n + part],
                )
            )
            copies[-1].start()
    for copy in copies:
        copy.wait()


def place(pieces, half, yh, core, sources, shape, out=None):
    extra = [] if out is None else [out]
    return pl.pallas_call(
        functools.partial(place_kernel, pieces, half),
        out_shape=jax.ShapeDtypeStruct(shape, jnp.bfloat16),
        in_specs=[pl.BlockSpec(memory_space=SMEM)] * 2
        + [pl.BlockSpec(memory_space=VMEM)] * len(sources)
        + [pl.BlockSpec(memory_space=HBM)] * len(extra),
        out_specs=pl.BlockSpec(memory_space=HBM),
        scratch_shapes=[pltpu.SemaphoreType.DMA((2 * len(sources),))],
        input_output_aliases={2 + len(sources): 0} if extra else {},
        compiler_params=PARAMS,
        cost_estimate=pl.CostEstimate(flops=0, bytes_accessed=2 ** 20, transcendentals=0),
    )(yh, core, *sources, *extra)


SWAP = [(0, 1), (1, 0)]


def shards(spectra, shot_weight):
    _, shots, bins, chans = spectra.shape
    depth = lax.axis_size("z")
    planes = lax.axis_size("y") * lax.axis_size("x")
    cores = lax.axis_size("c")
    factor = (shots * planes * cores) ** (-0.5)
    core = lax.axis_index("c").astype(jnp.int32).reshape(1)
    yh = lax.axis_index("yh").astype(jnp.int32).reshape(1)
    lanes = 2 * chans
    k_rows = planes * shots
    rows = depth * chans
    width = 2 * (rows // 2)

    turned = jnp.swapaxes(spectra, 2, 3)
    scaled = vmem_call(
        scale_kernel,
        jax.ShapeDtypeStruct((depth, planes, shots, lanes), jnp.bfloat16),
        [HBM, HBM],
        [
            pltpu.SMEM((shots,), jnp.float32),
            pltpu.VMEM((2, shots, chans, bins), jnp.bfloat16),
            pltpu.VMEM((planes, depth, shots, lanes), jnp.float32),
            pltpu.SemaphoreType.DMA((STEPS + 1,)),
        ],
        nbytes=2 * spectra.size * 2,
        params=pltpu.CompilerParams(vmem_limit_bytes=56 * 1024 * 1024),
    )(shot_weight, turned)
    scaled = scaled.reshape(bins, shots, lanes)
    mine = lax.all_to_all(scaled, ("z", "y", "x"), 0, 0, tiled=True)
    half = bins // cores
    first = lax.axis_index("c") * half
    far = lax.ppermute(lax.dynamic_slice_in_dim(mine, first, half), "yh", SWAP)
    near = lax.ppermute(mine, "c", SWAP)

    flops = 2 * rows * 4 * k_rows * width
    own, left = vmem_call(
        functools.partial(own_kernel, factor),
        (
            jax.ShapeDtypeStruct((rows, width), jnp.bfloat16),
            jax.ShapeDtypeStruct((rows, 4 * k_rows), jnp.bfloat16),
        ),
        [SMEM, VMEM, VMEM],
        [pltpu.VMEM((4 * k_rows, width), jnp.bfloat16)],
        flops=flops,
        nbytes=4 * rows * width * 2,
    )(core, mine.reshape(depth, k_rows, lanes), near.reshape(depth, k_rows, lanes))
    own, near = lax.optimization_barrier((own, near))
    far_other = lax.ppermute(lax.dynamic_slice_in_dim(near, first, half), "yh", SWAP)
    own = lax.all_to_all(own.reshape(depth, chans, width), "z", 0, 0, tiled=True)
    half_right = [pltpu.VMEM((2 * k_rows, width), jnp.bfloat16)]
    part = (depth // cores, k_rows, lanes)
    cross = vmem_call(
        first_kernel,
        jax.ShapeDtypeStruct((rows, width), jnp.float32),
        [VMEM, VMEM],
        half_right,
        flops=15 * flops,
    )(left, far.reshape(part))
    own, cross, far_other = lax.optimization_barrier((own, cross, far_other))
    per = depth // cores
    shape = (2, per, chans, 2 * rows)
    theirs = (1 - lax.axis_index("c")) * per
    own_other = lax.ppermute(lax.dynamic_slice_in_dim(own, theirs, per), "c", SWAP)
    cross = vmem_call(
        functools.partial(second_kernel, factor),
        jax.ShapeDtypeStruct((rows, width), jnp.bfloat16),
        [VMEM, VMEM, VMEM],
        half_right,
        flops=flops,
        nbytes=4 * rows * width * 2,
    )(left, far_other.reshape(part), cross)
    cross = lax.all_to_all(cross.reshape(depth, chans, width), "z", 0, 0, tiled=True)
    out = place((0, 1), 0, yh, core, (own, own_other), shape)
    out, cross = lax.optimization_barrier((out, cross))
    cross_other = lax.ppermute(lax.dynamic_slice_in_dim(cross, theirs, per), "c", SWAP)
    out = place((0,), 1, yh, core, (cross,), shape, out)
    return place((1,), 1, yh, core, (cross_other,), shape, out)


def solution(mesh):
    fine = Mesh(mesh.devices.reshape(4, 4, 2, 2, 8), ("y", "x", "c", "yh", "z"))
    shot, pair = ("y", "x", "c"), ("yh", "z")
    return jax.shard_map(
        shards,
        mesh=fine,
        in_specs=(P(None, shot, None, pair), P(shot)),
        out_specs=P(None, shot, pair, None),
        check_vma=False,
    )
```

```python
import functools

import jax
import jax.numpy as jnp
from jax import lax
from jax.experimental import pallas as pl
from jax.experimental.pallas import tpu as pltpu
from jax.sharding import Mesh, PartitionSpec as P

VMEM = pltpu.MemorySpace.VMEM
SMEM = pltpu.MemorySpace.SMEM
HBM = pltpu.MemorySpace.HBM
STEPS = 4
PARAMS = pltpu.CompilerParams(vmem_limit_bytes=32 * 1024 * 1024)


def vmem_call(body, out_shape, in_spaces, scratch=(), flops=0, nbytes=0, params=PARAMS):
    outs = out_shape if isinstance(out_shape, (list, tuple)) else (out_shape,)
    specs = [pl.BlockSpec(memory_space=VMEM) for _ in outs]
    return pl.pallas_call(
        body,
        out_shape=out_shape,
        in_specs=[pl.BlockSpec(memory_space=s) for s in in_spaces],
        out_specs=specs if isinstance(out_shape, (list, tuple)) else specs[0],
        scratch_shapes=list(scratch),
        compiler_params=params,
        cost_estimate=pl.CostEstimate(flops=flops, bytes_accessed=nbytes, transcendentals=0),
    )


def scale_kernel(weight_hbm, x_hbm, out_ref, weight_ref, x_ref, turned, sems):
    _, shots, chans, bins = x_ref.shape
    planes, cores, depth = turned.shape[:3]
    step = shots // STEPS
    weight_copy = pltpu.make_async_copy(weight_hbm, weight_ref, sems.at[STEPS])
    weight_copy.start()
    copies = []
    for i in range(STEPS):
        some = pl.ds(i * step, step)
        copies.append(pltpu.make_async_copy(x_hbm.at[:, some], x_ref.at[:, some], sems.at[i]))
        copies[-1].start()
    weight_copy.wait()
    for s in range(shots):
        if s % step == 0:
            copies[s // step].wait()
        block = x_ref[:, s].reshape(2 * chans, bins).astype(jnp.float32) * weight_ref[s]
        block = block.astype(jnp.bfloat16).astype(jnp.float32)
        turned[:, :, :, s, :] = block.T.reshape(planes, cores, depth, 2 * chans)
    for z in range(depth):
        out_ref[z] = turned[:, :, z].astype(jnp.bfloat16)


def split_parts(first, second):
    half = first.shape[1] // 2
    p = jnp.concatenate([first[:, :half], second[:, :half]], axis=1)
    q = jnp.concatenate([first[:, half:], second[:, half:]], axis=1)
    return p, q


def fill_right(right, pairs):
    width, k_rows = right.shape[1] // 2, right.shape[0] // 2
    for j, (first, second) in enumerate(pairs):
        p, q = split_parts(first, second)
        cols = slice(j * 128, (j + 1) * 128)
        icols = slice(width + j * 128, width + (j + 1) * 128)
        right[:k_rows, cols] = p
        right[:k_rows, icols] = q
        right[k_rows:, cols] = q
        right[k_rows:, icols] = -p


def multiply(left_ref, right, out_ref, factor):
    rows, step = left_ref.shape[0], 256
    for r in range(rows // step):
        some = slice(r * step, (r + 1) * step)
        acc = jnp.dot(left_ref[some, :], right[...], preferred_element_type=jnp.float32)
        out_ref[some, :] = (acc * factor).astype(jnp.bfloat16)


def own_kernel(factor, zl_ref, mine_ref, near_ref, out_ref, left_ref, right):
    blocks, k_rows, _ = mine_ref.shape
    for zl in range(2):

        @pl.when(zl_ref[0] == zl)
        def _(zl=zl):
            even, odd = (mine_ref, near_ref) if zl == 0 else (near_ref, mine_ref)
            for j in range(blocks):
                p, q = split_parts(even[j], odd[j])
                rows = slice(j * 128, (j + 1) * 128)
                left_ref[rows, :k_rows] = p.T
                left_ref[rows, k_rows:] = q.T
            half = blocks // 2
            fill_right(right, [(even[j], odd[j]) for j in range(zl * half, (zl + 1) * half)])

    multiply(left_ref, right, out_ref, factor)


def right_kernel(far_ref, right):
    fill_right(right, [(far_ref[j], far_ref[j + 1]) for j in range(0, far_ref.shape[0], 2)])


def cross_kernel(factor, left_ref, right, out_ref):
    multiply(left_ref, right, out_ref, factor)


def place_own_kernel(yh_ref, source, out_hbm, sems):
    width = out_hbm.shape[3] // 4
    copies = []
    for quarter in range(2):
        column = pl.multiple_of((2 * yh_ref[0] + quarter) * width, width)
        for part in range(2):
            copies.append(
                pltpu.make_async_copy(
                    source.at[:, quarter, :, pl.ds(part * width, width)],
                    out_hbm.at[part, :, :, pl.ds(column, width)],
                    sems.at[2 * quarter + part],
                )
            )
            copies[-1].start()
    for copy in copies:
        copy.wait()


def place_cross_kernel(yh_ref, source, _, out_hbm, turned, sems):
    bins, _, rows, wide = source.shape
    width = wide // 2
    column = pl.multiple_of((1 - yh_ref[0]) * 2 * width, 2 * width)
    copies = []
    for part in range(2):
        for b in range(bins):
            for j in range(width // 64):
                cols = slice(part * width + j * 64, part * width + (j + 1) * 64)
                turned[part, b, :, j * 128:(j + 1) * 128] = jnp.concatenate(
                    [source[b, 0, :, cols], source[b, 1, :, cols]], axis=1
                )
        copies.append(
            pltpu.make_async_copy(
                turned.at[part],
                out_hbm.at[part, :, :, pl.ds(column, 2 * width)],
                sems.at[part],
            )
        )
        copies[-1].start()
    for copy in copies:
        copy.wait()


def place(body, yh, source, shape, scratch, out=None):
    extra = [] if out is None else [out]
    return pl.pallas_call(
        body,
        out_shape=jax.ShapeDtypeStruct(shape, jnp.bfloat16),
        in_specs=[pl.BlockSpec(memory_space=SMEM), pl.BlockSpec(memory_space=VMEM)]
        + [pl.BlockSpec(memory_space=HBM)] * len(extra),
        out_specs=pl.BlockSpec(memory_space=HBM),
        scratch_shapes=scratch,
        input_output_aliases={2: 0} if extra else {},
        compiler_params=PARAMS,
        cost_estimate=pl.CostEstimate(flops=0, bytes_accessed=2 ** 20, transcendentals=0),
    )(yh, source, *extra)


SWAP = [(0, 1), (1, 0)]


def shards(spectra, shot_weight):
    _, shots, bins, chans = spectra.shape
    depth = lax.axis_size("zh")
    planes = lax.axis_size("y") * lax.axis_size("x")
    cores = lax.axis_size("c")
    k_rows = planes * cores * shots
    factor = k_rows ** (-0.5)
    yh = lax.axis_index("yh").astype(jnp.int32).reshape(1)
    zl = lax.axis_index("zl").astype(jnp.int32).reshape(1)
    lanes = 2 * chans
    rows = 2 * depth * chans
    width = rows
    blocks = (depth, k_rows, lanes)

    turned = jnp.swapaxes(spectra, 2, 3)
    scaled = vmem_call(
        scale_kernel,
        jax.ShapeDtypeStruct((depth, planes, cores, shots, lanes), jnp.bfloat16),
        [HBM, HBM],
        [
            pltpu.SMEM((shots,), jnp.float32),
            pltpu.VMEM((2, shots, chans, bins), jnp.bfloat16),
            pltpu.VMEM((planes, cores, depth, shots, lanes), jnp.float32),
            pltpu.SemaphoreType.DMA((STEPS + 1,)),
        ],
        nbytes=2 * spectra.size * 2,
        params=pltpu.CompilerParams(vmem_limit_bytes=56 * 1024 * 1024),
    )(shot_weight, turned)
    scaled = scaled.reshape(bins, shots, lanes)
    mine = lax.all_to_all(scaled, ("zh", "y", "x", "c"), 0, 0, tiled=True)
    near = lax.ppermute(mine, "zl", SWAP)
    far = lax.ppermute(mine, "yh", SWAP)

    flops = 2 * rows * 2 * k_rows * width
    own, left = vmem_call(
        functools.partial(own_kernel, factor),
        (
            jax.ShapeDtypeStruct((rows, width), jnp.bfloat16),
            jax.ShapeDtypeStruct((rows, 2 * k_rows), jnp.bfloat16),
        ),
        [SMEM, VMEM, VMEM],
        [pltpu.VMEM((2 * k_rows, width), jnp.bfloat16)],
        flops=flops,
        nbytes=4 * rows * width * 2,
    )(zl, mine.reshape(blocks), near.reshape(blocks))
    pieces = (2 * depth, chans, width)
    own = lax.all_to_all(own.reshape(pieces), ("zh", "zl"), 0, 0, tiled=True)

    right = vmem_call(
        right_kernel,
        jax.ShapeDtypeStruct((2 * k_rows, width), jnp.bfloat16),
        [VMEM],
        flops=40 * flops,
    )(far.reshape(blocks))
    own, right = lax.optimization_barrier((own, right))
    cross = vmem_call(
        functools.partial(cross_kernel, factor),
        jax.ShapeDtypeStruct((rows, width), jnp.bfloat16),
        [VMEM, VMEM],
        flops=flops,
        nbytes=4 * rows * width * 2,
    )(left, right)
    cross = lax.all_to_all(cross.reshape(pieces), ("zh", "zl"), 0, 0, tiled=True)

    shape = (2, depth, chans, 2 * rows)
    by_bin = (depth, 2, chans, width)
    out = place(place_own_kernel, yh, own.reshape(by_bin), shape, [pltpu.SemaphoreType.DMA((4,))])
    out, cross = lax.optimization_barrier((out, cross))
    scratch = [
        pltpu.VMEM((2, depth, chans, width), jnp.bfloat16),
        pltpu.SemaphoreType.DMA((2,)),
    ]
    return place(place_cross_kernel, yh, cross.reshape(by_bin), shape, scratch, out)


def solution(mesh):
    fine = Mesh(mesh.devices.reshape(4, 4, 2, 2, 4, 2), ("y", "x", "c", "yh", "zh", "zl"))
    shot, pair = ("y", "x", "c"), ("yh", "zh", "zl")
    return jax.shard_map(
        shards,
        mesh=fine,
        in_specs=(P(None, shot, None, pair), P(shot)),
        out_specs=P(None, shot, pair, None),
        check_vma=False,
    )
```

```python
import functools

import jax
import jax.numpy as jnp
from jax import lax
from jax.experimental import pallas as pl
from jax.experimental.pallas import tpu as pltpu
from jax.sharding import Mesh, PartitionSpec as P

VMEM = pltpu.MemorySpace.VMEM
SMEM = pltpu.MemorySpace.SMEM
HBM = pltpu.MemorySpace.HBM
STEPS = 4
PARAMS = pltpu.CompilerParams(vmem_limit_bytes=32 * 1024 * 1024)


def vmem_call(body, out_shape, in_spaces, scratch=(), flops=0, nbytes=0, params=PARAMS):
    outs = out_shape if isinstance(out_shape, (list, tuple)) else (out_shape,)
    specs = [pl.BlockSpec(memory_space=VMEM) for _ in outs]
    return pl.pallas_call(
        body,
        out_shape=out_shape,
        in_specs=[pl.BlockSpec(memory_space=s) for s in in_spaces],
        out_specs=specs if isinstance(out_shape, (list, tuple)) else specs[0],
        scratch_shapes=list(scratch),
        compiler_params=params,
        cost_estimate=pl.CostEstimate(flops=flops, bytes_accessed=nbytes, transcendentals=0),
    )


def scale_kernel(weight_hbm, x_hbm, out_ref, weight_ref, x_ref, turned, sems):
    _, shots, chans, bins = x_ref.shape
    planes, cores, depth = turned.shape[:3]
    step = shots // STEPS
    weight_copy = pltpu.make_async_copy(weight_hbm, weight_ref, sems.at[STEPS])
    weight_copy.start()
    copies = []
    for i in range(STEPS):
        some = pl.ds(i * step, step)
        copies.append(pltpu.make_async_copy(x_hbm.at[:, some], x_ref.at[:, some], sems.at[i]))
        copies[-1].start()
    weight_copy.wait()
    for s in range(shots):
        if s % step == 0:
            copies[s // step].wait()
        block = x_ref[:, s].reshape(2 * chans, bins).astype(jnp.float32) * weight_ref[s]
        block = block.astype(jnp.bfloat16).astype(jnp.float32)
        turned[:, :, :, s, :] = block.T.reshape(planes, cores, depth, 2 * chans)
    for z in range(depth):
        out_ref[z] = turned[:, :, z].astype(jnp.bfloat16)


def split_parts(first, second):
    half = first.shape[1] // 2
    p = jnp.concatenate([first[:, :half], second[:, :half]], axis=1)
    q = jnp.concatenate([first[:, half:], second[:, half:]], axis=1)
    return p, q


def fill_right(right, pairs):
    width, k_rows = right.shape[1] // 2, right.shape[0] // 2
    for j, (first, second) in enumerate(pairs):
        p, q = split_parts(first, second)
        cols = slice(j * 128, (j + 1) * 128)
        icols = slice(width + j * 128, width + (j + 1) * 128)
        right[:k_rows, cols] = p
        right[:k_rows, icols] = q
        right[k_rows:, cols] = q
        right[k_rows:, icols] = -p


def block_pairs(ref):
    return [(ref[j], ref[j + 1]) for j in range(0, ref.shape[0], 2)]


def fill_left(left_ref, ref):
    k_rows = ref.shape[1]
    for j, (first, second) in enumerate(block_pairs(ref)):
        p, q = split_parts(first, second)
        rows = slice(j * 128, (j + 1) * 128)
        left_ref[rows, :k_rows] = p.T
        left_ref[rows, k_rows:] = q.T


def rows_of(left_ref, right_ref, factor):
    acc = jnp.dot(left_ref[...], right_ref[...], preferred_element_type=jnp.float32)
    return (acc * factor).astype(jnp.bfloat16)


def begin_kernel(factor, mine_ref, out_ref, left_ref, right_ref):
    fill_left(left_ref, mine_ref)
    fill_right(right_ref, block_pairs(mine_ref))
    out_ref[...] = rows_of(left_ref, right_ref, factor).reshape(out_ref.shape)


def own_kernel(factor, zl_ref, near_ref, right_ref, begun_ref, out_ref, left_ref):
    zl = zl_ref[0]
    fill_left(left_ref, near_ref)
    theirs = rows_of(left_ref, right_ref, factor).reshape(begun_ref.shape)
    for j in range(begun_ref.shape[0]):
        out_ref[2 * j + zl] = begun_ref[j]
        out_ref[2 * j + 1 - zl] = theirs[j]


def cross_kernel(factor, zl_ref, left_ref, left_near_ref, far_ref, out_ref, right):
    zl = zl_ref[0]
    fill_right(right, block_pairs(far_ref))
    half = (out_ref.shape[0] // 2,) + out_ref.shape[1:]
    for ref, parity in ((left_ref, zl), (left_near_ref, 1 - zl)):
        block = rows_of(ref, right, factor).reshape(half)
        for j in range(half[0]):
            out_ref[2 * j + parity] = block[j]


def place_kernel(half, yh_ref, source, *refs):
    out_hbm, turned, sems = refs[-3:]
    bins, _, rows, wide = source.shape
    width = wide // 2
    column = pl.multiple_of((yh_ref[0] + half) % 2 * 2 * width, 2 * width)
    copies = []
    for part in range(2):
        for b in range(bins):
            for j in range(width // 64):
                cols = slice(part * width + j * 64, part * width + (j + 1) * 64)
                turned[part, b, :, j * 128:(j + 1) * 128] = jnp.concatenate(
                    [source[b, 0, :, cols], source[b, 1, :, cols]], axis=1
                )
        copies.append(
            pltpu.make_async_copy(
                turned.at[part],
                out_hbm.at[part, :, :, pl.ds(column, 2 * width)],
                sems.at[part],
            )
        )
        copies[-1].start()
    for copy in copies:
        copy.wait()


def place(half, yh, source, shape, scratch, out=None):
    extra = [] if out is None else [out]
    return pl.pallas_call(
        functools.partial(place_kernel, half),
        out_shape=jax.ShapeDtypeStruct(shape, jnp.bfloat16),
        in_specs=[pl.BlockSpec(memory_space=SMEM), pl.BlockSpec(memory_space=VMEM)]
        + [pl.BlockSpec(memory_space=HBM)] * len(extra),
        out_specs=pl.BlockSpec(memory_space=HBM),
        scratch_shapes=scratch,
        input_output_aliases={2: 0} if extra else {},
        compiler_params=PARAMS,
        cost_estimate=pl.CostEstimate(flops=0, bytes_accessed=2 ** 20, transcendentals=0),
    )(yh, source, *extra)


SWAP = [(0, 1), (1, 0)]


def shards(spectra, shot_weight):
    _, shots, bins, chans = spectra.shape
    depth = lax.axis_size("zh")
    planes = lax.axis_size("y") * lax.axis_size("x")
    cores = lax.axis_size("c")
    k_rows = planes * cores * shots
    factor = k_rows ** (-0.5)
    yh = lax.axis_index("yh").astype(jnp.int32).reshape(1)
    zl = lax.axis_index("zl").astype(jnp.int32).reshape(1)
    lanes = 2 * chans
    rows = 2 * depth * chans
    width = rows
    blocks = (depth, k_rows, lanes)

    turned = jnp.swapaxes(spectra, 2, 3)
    scaled = vmem_call(
        scale_kernel,
        jax.ShapeDtypeStruct((depth, planes, cores, shots, lanes), jnp.bfloat16),
        [HBM, HBM],
        [
            pltpu.SMEM((shots,), jnp.float32),
            pltpu.VMEM((2, shots, chans, bins), jnp.bfloat16),
            pltpu.VMEM((planes, cores, depth, shots, lanes), jnp.float32),
            pltpu.SemaphoreType.DMA((STEPS + 1,)),
        ],
        nbytes=2 * spectra.size * 2,
        params=pltpu.CompilerParams(vmem_limit_bytes=56 * 1024 * 1024),
    )(shot_weight, turned)
    scaled = scaled.reshape(bins, shots, lanes)
    mine = lax.all_to_all(scaled, ("zh", "y", "x", "c"), 0, 0, tiled=True)
    near = lax.ppermute(mine, "zl", SWAP)
    far = lax.ppermute(mine, "yh", SWAP)

    flops = 2 * rows * 2 * k_rows * width
    left_shape = jax.ShapeDtypeStruct((rows // 2, 2 * k_rows), jnp.bfloat16)
    right_shape = jax.ShapeDtypeStruct((2 * k_rows, width), jnp.bfloat16)
    begun, left, right = vmem_call(
        functools.partial(begin_kernel, factor),
        (jax.ShapeDtypeStruct((depth, chans, width), jnp.bfloat16), left_shape, right_shape),
        [VMEM],
        flops=flops // 2,
    )(mine.reshape(blocks))
    pieces = (2 * depth, chans, width)
    own, left_near = vmem_call(
        functools.partial(own_kernel, factor),
        (jax.ShapeDtypeStruct(pieces, jnp.bfloat16), left_shape),
        [SMEM, VMEM, VMEM, VMEM],
        flops=flops // 2,
    )(zl, near.reshape(blocks), right, begun)
    own = lax.all_to_all(own, ("zh", "zl"), 0, 0, tiled=True)

    cross = vmem_call(
        functools.partial(cross_kernel, factor),
        jax.ShapeDtypeStruct(pieces, jnp.bfloat16),
        [SMEM, VMEM, VMEM, VMEM],
        [pltpu.VMEM((2 * k_rows, width), jnp.bfloat16)],
        flops=40 * flops,
        nbytes=4 * rows * width * 2,
    )(zl, left, left_near, far.reshape(blocks))
    own, cross = lax.optimization_barrier((own, cross))
    cross = lax.all_to_all(cross, ("zh", "zl"), 0, 0, tiled=True)

    shape = (2, depth, chans, 2 * rows)
    by_bin = (depth, 2, chans, width)
    scratch = [
        pltpu.VMEM((2, depth, chans, width), jnp.bfloat16),
        pltpu.SemaphoreType.DMA((2,)),
    ]
    out = place(0, yh, own.reshape(by_bin), shape, scratch)
    out, cross = lax.optimization_barrier((out, cross))
    return place(1, yh, cross.reshape(by_bin), shape, scratch, out)


def solution(mesh):
    fine = Mesh(mesh.devices.reshape(4, 4, 2, 2, 4, 2), ("y", "x", "c", "yh", "zh", "zl"))
    shot, pair = ("y", "x", "c"), ("yh", "zh", "zl")
    return jax.shard_map(
        shards,
        mesh=fine,
        in_specs=(P(None, shot, None, pair), P(shot)),
        out_specs=P(None, shot, pair, None),
        check_vma=False,
    )
```

```python
import functools

import jax
import jax.numpy as jnp
from jax import lax
from jax.experimental import pallas as pl
from jax.experimental.pallas import tpu as pltpu
from jax.sharding import Mesh, PartitionSpec as P

VMEM = pltpu.MemorySpace.VMEM
SMEM = pltpu.MemorySpace.SMEM
HBM = pltpu.MemorySpace.HBM
STEPS = 4
PARAMS = pltpu.CompilerParams(vmem_limit_bytes=32 * 1024 * 1024)


def vmem_call(body, out_shape, in_spaces, scratch=(), flops=0, nbytes=0, params=PARAMS):
    outs = out_shape if isinstance(out_shape, (list, tuple)) else (out_shape,)
    specs = [pl.BlockSpec(memory_space=VMEM) for _ in outs]
    return pl.pallas_call(
        body,
        out_shape=out_shape,
        in_specs=[pl.BlockSpec(memory_space=s) for s in in_spaces],
        out_specs=specs if isinstance(out_shape, (list, tuple)) else specs[0],
        scratch_shapes=list(scratch),
        compiler_params=params,
        cost_estimate=pl.CostEstimate(flops=flops, bytes_accessed=nbytes, transcendentals=0),
    )


def scale_kernel(weight_hbm, x_hbm, out_ref, weight_ref, x_ref, turned, sems):
    _, shots, chans, bins = x_ref.shape
    planes, cores, depth = turned.shape[:3]
    step = shots // STEPS
    weight_copy = pltpu.make_async_copy(weight_hbm, weight_ref, sems.at[STEPS])
    weight_copy.start()
    copies = []
    for i in range(STEPS):
        some = pl.ds(i * step, step)
        copies.append(pltpu.make_async_copy(x_hbm.at[:, some], x_ref.at[:, some], sems.at[i]))
        copies[-1].start()
    weight_copy.wait()
    for s in range(shots):
        if s % step == 0:
            copies[s // step].wait()
        block = x_ref[:, s].reshape(2 * chans, bins).astype(jnp.float32) * weight_ref[s]
        block = block.astype(jnp.bfloat16).T.astype(jnp.float32)
        turned[:, :, :, s, :] = block.reshape(planes, cores, depth, 2 * chans)
    for z in range(depth):
        for core in range(cores):
            out_ref[z, core] = turned[:, core, z].astype(jnp.bfloat16)


def split_parts(first, second):
    half = first.shape[1] // 2
    p = jnp.concatenate([first[:, :half], second[:, :half]], axis=1)
    q = jnp.concatenate([first[:, half:], second[:, half:]], axis=1)
    return p, q


def fill_right(right, pairs):
    width, k_rows = right.shape[1] // 2, right.shape[0] // 2
    for j, (first, second) in enumerate(pairs):
        p, q = split_parts(first, second)
        cols = slice(j * 128, (j + 1) * 128)
        icols = slice(width + j * 128, width + (j + 1) * 128)
        right[:k_rows, cols] = p
        right[:k_rows, icols] = q
        right[k_rows:, cols] = q
        right[k_rows:, icols] = -p


def block_pairs(ref):
    return [(ref[j], ref[j + 1]) for j in range(0, ref.shape[0], 2)]


def fill_left(left_ref, ref):
    k_rows = ref.shape[1]
    for j, (first, second) in enumerate(block_pairs(ref)):
        p, q = split_parts(first, second)
        rows = slice(j * 128, (j + 1) * 128)
        left_ref[rows, :k_rows] = p.T
        left_ref[rows, k_rows:] = q.T


def rows_of(left_ref, right_ref, factor):
    acc = jnp.dot(left_ref[...], right_ref[...], preferred_element_type=jnp.float32)
    return (acc * factor).astype(jnp.bfloat16)


def begin_kernel(factor, mine_ref, out_ref, left_ref, right_ref):
    fill_left(left_ref, mine_ref)
    fill_right(right_ref, block_pairs(mine_ref))
    out_ref[...] = rows_of(left_ref, right_ref, factor).reshape(out_ref.shape)


def own_kernel(factor, zl_ref, near_ref, right_ref, begun_ref, out_ref, left_ref):
    zl = zl_ref[0]
    fill_left(left_ref, near_ref)
    theirs = rows_of(left_ref, right_ref, factor).reshape(begun_ref.shape)
    for j in range(begun_ref.shape[0]):
        out_ref[2 * j + zl] = begun_ref[j]
        out_ref[2 * j + 1 - zl] = theirs[j]


def cross_kernel(factor, zl_ref, left_ref, left_near_ref, far_ref, out_ref, right):
    zl = zl_ref[0]
    fill_right(right, block_pairs(far_ref))
    half = (out_ref.shape[0] // 2,) + out_ref.shape[1:]
    for ref, parity in ((left_ref, zl), (left_near_ref, 1 - zl)):
        block = rows_of(ref, right, factor).reshape(half)
        for j in range(half[0]):
            out_ref[2 * j + parity] = block[j]


def place_kernel(half, yh_ref, source, *refs):
    out_hbm, turned, sems = refs[-3:]
    bins, _, rows, wide = source.shape
    width = wide // 2
    column = pl.multiple_of((yh_ref[0] + half) % 2 * 2 * width, 2 * width)
    copies = []
    for part in range(2):
        for b in range(bins):
            for j in range(width // 64):
                cols = slice(part * width + j * 64, part * width + (j + 1) * 64)
                turned[part, b, :, j * 128:(j + 1) * 128] = jnp.concatenate(
                    [source[b, 0, :, cols], source[b, 1, :, cols]], axis=1
                )
            copies.append(
                pltpu.make_async_copy(
                    turned.at[part, b],
                    out_hbm.at[part, b, :, pl.ds(column, 2 * width)],
                    sems.at[part * bins + b],
                )
            )
            copies[-1].start()
    for copy in copies:
        copy.wait()


def place(half, yh, source, shape, scratch, out=None):
    extra = [] if out is None else [out]
    return pl.pallas_call(
        functools.partial(place_kernel, half),
        out_shape=jax.ShapeDtypeStruct(shape, jnp.bfloat16),
        in_specs=[pl.BlockSpec(memory_space=SMEM), pl.BlockSpec(memory_space=VMEM)]
        + [pl.BlockSpec(memory_space=HBM)] * len(extra),
        out_specs=pl.BlockSpec(memory_space=HBM),
        scratch_shapes=scratch,
        input_output_aliases={2: 0} if extra else {},
        compiler_params=PARAMS,
        cost_estimate=pl.CostEstimate(flops=0, bytes_accessed=2 ** 20, transcendentals=0),
    )(yh, source, *extra)


SWAP = [(0, 1), (1, 0)]


def shards(spectra, shot_weight):
    _, shots, bins, chans = spectra.shape
    depth = lax.axis_size("zh")
    planes = lax.axis_size("y") * lax.axis_size("x")
    cores = lax.axis_size("c")
    k_rows = planes * cores * shots
    factor = k_rows ** (-0.5)
    yh = lax.axis_index("yh").astype(jnp.int32).reshape(1)
    zl = lax.axis_index("zl").astype(jnp.int32).reshape(1)
    lanes = 2 * chans
    rows = 2 * depth * chans
    width = rows
    blocks = (depth, k_rows, lanes)

    turned = jnp.swapaxes(spectra, 2, 3)
    scaled = vmem_call(
        scale_kernel,
        jax.ShapeDtypeStruct((depth, cores, planes, shots, lanes), jnp.bfloat16),
        [HBM, HBM],
        [
            pltpu.SMEM((shots,), jnp.float32),
            pltpu.VMEM((2, shots, chans, bins), jnp.bfloat16),
            pltpu.VMEM((planes, cores, depth, shots, lanes), jnp.float32),
            pltpu.SemaphoreType.DMA((STEPS + 1,)),
        ],
        nbytes=2 * spectra.size * 2,
        params=pltpu.CompilerParams(vmem_limit_bytes=56 * 1024 * 1024),
    )(shot_weight, turned)
    scaled = scaled.reshape(bins, shots, lanes)
    mine = lax.all_to_all(scaled, ("zh", "c", "y", "x"), 0, 0, tiled=True)
    near = lax.ppermute(mine, "zl", SWAP)
    far = lax.ppermute(mine, "yh", SWAP)

    flops = 2 * rows * 2 * k_rows * width
    left_shape = jax.ShapeDtypeStruct((rows // 2, 2 * k_rows), jnp.bfloat16)
    right_shape = jax.ShapeDtypeStruct((2 * k_rows, width), jnp.bfloat16)
    begun, left, right = vmem_call(
        functools.partial(begin_kernel, factor),
        (jax.ShapeDtypeStruct((depth, chans, width), jnp.bfloat16), left_shape, right_shape),
        [VMEM],
        flops=flops // 2,
    )(mine.reshape(blocks))
    pieces = (2 * depth, chans, width)
    own, left_near = vmem_call(
        functools.partial(own_kernel, factor),
        (jax.ShapeDtypeStruct(pieces, jnp.bfloat16), left_shape),
        [SMEM, VMEM, VMEM, VMEM],
        flops=flops // 2,
    )(zl, near.reshape(blocks), right, begun)
    own = lax.all_to_all(own, ("zh", "zl"), 0, 0, tiled=True)

    cross = vmem_call(
        functools.partial(cross_kernel, factor),
        jax.ShapeDtypeStruct(pieces, jnp.bfloat16),
        [SMEM, VMEM, VMEM, VMEM],
        [pltpu.VMEM((2 * k_rows, width), jnp.bfloat16)],
        flops=40 * flops,
        nbytes=4 * rows * width * 2,
    )(zl, left, left_near, far.reshape(blocks))
    own, cross = lax.optimization_barrier((own, cross))
    cross = lax.all_to_all(cross, ("zh", "zl"), 0, 0, tiled=True)

    shape = (2, depth, chans, 2 * rows)
    by_bin = (depth, 2, chans, width)
    scratch = [
        pltpu.VMEM((2, depth, chans, width), jnp.bfloat16),
        pltpu.SemaphoreType.DMA((2 * depth,)),
    ]
    out = place(0, yh, own.reshape(by_bin), shape, scratch)
    out, cross = lax.optimization_barrier((out, cross))
    return place(1, yh, cross.reshape(by_bin), shape, scratch, out)


def solution(mesh):
    fine = Mesh(mesh.devices.reshape(4, 4, 2, 2, 4, 2), ("y", "x", "c", "yh", "zh", "zl"))
    shot, pair = ("y", "x", "c"), ("yh", "zh", "zl")
    return jax.shard_map(
        shards,
        mesh=fine,
        in_specs=(P(None, shot, None, pair), P(shot)),
        out_specs=P(None, shot, pair, None),
        check_vma=False,
    )
```

```python
import functools

import jax
import jax.numpy as jnp
from jax import lax
from jax.experimental import pallas as pl
from jax.experimental.pallas import tpu as pltpu
from jax.sharding import Mesh, PartitionSpec as P

VMEM = pltpu.MemorySpace.VMEM
SMEM = pltpu.MemorySpace.SMEM
HBM = pltpu.MemorySpace.HBM
STEPS = 8
PARAMS = pltpu.CompilerParams(vmem_limit_bytes=32 * 1024 * 1024)


def vmem_call(body, out_shape, in_spaces, scratch=(), flops=0, nbytes=0, params=PARAMS):
    outs = out_shape if isinstance(out_shape, (list, tuple)) else (out_shape,)
    specs = [pl.BlockSpec(memory_space=VMEM) for _ in outs]
    return pl.pallas_call(
        body,
        out_shape=out_shape,
        in_specs=[pl.BlockSpec(memory_space=s) for s in in_spaces],
        out_specs=specs if isinstance(out_shape, (list, tuple)) else specs[0],
        scratch_shapes=list(scratch),
        compiler_params=params,
        cost_estimate=pl.CostEstimate(flops=flops, bytes_accessed=nbytes, transcendentals=0),
    )


def scale_kernel(weight_hbm, x_hbm, out_ref, weight_ref, x_ref, turned, sems):
    _, shots, chans, bins = x_ref.shape
    planes, cores, depth = turned.shape[:3]
    step = shots // STEPS
    weight_copy = pltpu.make_async_copy(weight_hbm, weight_ref, sems.at[STEPS])
    weight_copy.start()
    copies = []
    for i in range(STEPS):
        some = pl.ds(i * step, step)
        copies.append(pltpu.make_async_copy(x_hbm.at[:, some], x_ref.at[:, some], sems.at[i]))
        copies[-1].start()
    weight_copy.wait()
    for s in range(shots):
        if s % step == 0:
            copies[s // step].wait()
        block = x_ref[:, s].reshape(2 * chans, bins).astype(jnp.float32) * weight_ref[s]
        block = block.astype(jnp.bfloat16).T.astype(jnp.float32)
        turned[:, :, :, s, :] = block.reshape(planes, cores, depth, 2 * chans)
    for z in range(depth):
        for core in range(cores):
            out_ref[z, core] = turned[:, core, z].astype(jnp.bfloat16)


def split_parts(first, second):
    half = first.shape[1] // 2
    p = jnp.concatenate([first[:, :half], second[:, :half]], axis=1)
    q = jnp.concatenate([first[:, half:], second[:, half:]], axis=1)
    return p, q


def fill_right(right, pairs):
    width, k_rows = right.shape[1] // 2, right.shape[0] // 2
    for j, (first, second) in enumerate(pairs):
        p, q = split_parts(first, second)
        cols = slice(j * 128, (j + 1) * 128)
        icols = slice(width + j * 128, width + (j + 1) * 128)
        right[:k_rows, cols] = p
        right[:k_rows, icols] = q
        right[k_rows:, cols] = q
        right[k_rows:, icols] = -p


def block_pairs(ref):
    return [(ref[j], ref[j + 1]) for j in range(0, ref.shape[0], 2)]


def fill_left(left_ref, ref):
    k_rows = ref.shape[1]
    for j, (first, second) in enumerate(block_pairs(ref)):
        p, q = split_parts(first, second)
        rows = slice(j * 128, (j + 1) * 128)
        left_ref[rows, :k_rows] = p.T
        left_ref[rows, k_rows:] = q.T


def rows_of(left_ref, right_ref, factor):
    acc = jnp.dot(left_ref[...], right_ref[...], preferred_element_type=jnp.float32)
    return (acc * factor).astype(jnp.bfloat16)


def begin_kernel(factor, mine_ref, out_ref, left_ref, right_ref):
    fill_left(left_ref, mine_ref)
    fill_right(right_ref, block_pairs(mine_ref))
    out_ref[...] = rows_of(left_ref, right_ref, factor).reshape(out_ref.shape)


def own_kernel(factor, zl_ref, near_ref, right_ref, begun_ref, out_ref, left_ref):
    zl = zl_ref[0]
    fill_left(left_ref, near_ref)
    theirs = rows_of(left_ref, right_ref, factor).reshape(begun_ref.shape)
    for j in range(begun_ref.shape[0]):
        out_ref[2 * j + zl] = begun_ref[j]
        out_ref[2 * j + 1 - zl] = theirs[j]


def cross_kernel(factor, zl_ref, left_ref, left_near_ref, far_ref, out_ref, right):
    zl = zl_ref[0]
    fill_right(right, block_pairs(far_ref))
    half = (out_ref.shape[0] // 2,) + out_ref.shape[1:]
    for ref, parity in ((left_ref, zl), (left_near_ref, 1 - zl)):
        block = rows_of(ref, right, factor).reshape(half)
        for j in range(half[0]):
            out_ref[2 * j + parity] = block[j]


def place_kernel(half, yh_ref, source, *refs):
    out_hbm, turned, sems = refs[-3:]
    bins, _, rows, wide = source.shape
    width = wide // 2
    column = pl.multiple_of((yh_ref[0] + half) % 2 * 2 * width, 2 * width)
    copies = []
    for part in range(2):
        for b in range(bins):
            for j in range(width // 64):
                cols = slice(part * width + j * 64, part * width + (j + 1) * 64)
                turned[part, b, :, j * 128:(j + 1) * 128] = jnp.concatenate(
                    [source[b, 0, :, cols], source[b, 1, :, cols]], axis=1
                )
            copies.append(
                pltpu.make_async_copy(
                    turned.at[part, b],
                    out_hbm.at[part, b, :, pl.ds(column, 2 * width)],
                    sems.at[part * bins + b],
                )
            )
            copies[-1].start()
    for copy in copies:
        copy.wait()


def place(half, yh, source, shape, scratch, out=None):
    extra = [] if out is None else [out]
    return pl.pallas_call(
        functools.partial(place_kernel, half),
        out_shape=jax.ShapeDtypeStruct(shape, jnp.bfloat16),
        in_specs=[pl.BlockSpec(memory_space=SMEM), pl.BlockSpec(memory_space=VMEM)]
        + [pl.BlockSpec(memory_space=HBM)] * len(extra),
        out_specs=pl.BlockSpec(memory_space=HBM),
        scratch_shapes=scratch,
        input_output_aliases={2: 0} if extra else {},
        compiler_params=PARAMS,
        cost_estimate=pl.CostEstimate(flops=0, bytes_accessed=2 ** 20, transcendentals=0),
    )(yh, source, *extra)


SWAP = [(0, 1), (1, 0)]


def shards(spectra, shot_weight):
    _, shots, bins, chans = spectra.shape
    depth = lax.axis_size("zh")
    planes = lax.axis_size("y") * lax.axis_size("x")
    cores = lax.axis_size("c")
    k_rows = planes * cores * shots
    factor = k_rows ** (-0.5)
    yh = lax.axis_index("yh").astype(jnp.int32).reshape(1)
    zl = lax.axis_index("zl").astype(jnp.int32).reshape(1)
    lanes = 2 * chans
    rows = 2 * depth * chans
    width = rows
    blocks = (depth, k_rows, lanes)

    turned = jnp.swapaxes(spectra, 2, 3)
    scaled = vmem_call(
        scale_kernel,
        jax.ShapeDtypeStruct((depth, cores, planes, shots, lanes), jnp.bfloat16),
        [HBM, HBM],
        [
            pltpu.SMEM((shots,), jnp.float32),
            pltpu.VMEM((2, shots, chans, bins), jnp.bfloat16),
            pltpu.VMEM((planes, cores, depth, shots, lanes), jnp.float32),
            pltpu.SemaphoreType.DMA((STEPS + 1,)),
        ],
        nbytes=2 * spectra.size * 2,
        params=pltpu.CompilerParams(vmem_limit_bytes=56 * 1024 * 1024),
    )(shot_weight, turned)
    scaled = scaled.reshape(bins, shots, lanes)
    mine = lax.all_to_all(scaled, ("zh", "c", "y", "x"), 0, 0, tiled=True)
    near = lax.ppermute(mine, "zl", SWAP)
    far = lax.ppermute(mine, "yh", SWAP)

    flops = 2 * rows * 2 * k_rows * width
    left_shape = jax.ShapeDtypeStruct((rows // 2, 2 * k_rows), jnp.bfloat16)
    right_shape = jax.ShapeDtypeStruct((2 * k_rows, width), jnp.bfloat16)
    begun, left, right = vmem_call(
        functools.partial(begin_kernel, factor),
        (jax.ShapeDtypeStruct((depth, chans, width), jnp.bfloat16), left_shape, right_shape),
        [VMEM],
        flops=flops // 2,
    )(mine.reshape(blocks))
    pieces = (2 * depth, chans, width)
    own, left_near = vmem_call(
        functools.partial(own_kernel, factor),
        (jax.ShapeDtypeStruct(pieces, jnp.bfloat16), left_shape),
        [SMEM, VMEM, VMEM, VMEM],
        flops=flops // 2,
    )(zl, near.reshape(blocks), right, begun)
    own = lax.all_to_all(own, ("zh", "zl"), 0, 0, tiled=True)

    cross = vmem_call(
        functools.partial(cross_kernel, factor),
        jax.ShapeDtypeStruct(pieces, jnp.bfloat16),
        [SMEM, VMEM, VMEM, VMEM],
        [pltpu.VMEM((2 * k_rows, width), jnp.bfloat16)],
        flops=40 * flops,
        nbytes=4 * rows * width * 2,
    )(zl, left, left_near, far.reshape(blocks))
    own, cross = lax.optimization_barrier((own, cross))
    cross = lax.all_to_all(cross, ("zh", "zl"), 0, 0, tiled=True)

    shape = (2, depth, chans, 2 * rows)
    by_bin = (depth, 2, chans, width)
    scratch = [
        pltpu.VMEM((2, depth, chans, width), jnp.bfloat16),
        pltpu.SemaphoreType.DMA((2 * depth,)),
    ]
    out = place(0, yh, own.reshape(by_bin), shape, scratch)
    out, cross = lax.optimization_barrier((out, cross))
    return place(1, yh, cross.reshape(by_bin), shape, scratch, out)


def solution(mesh):
    fine = Mesh(mesh.devices.reshape(4, 4, 2, 2, 4, 2), ("y", "x", "c", "yh", "zh", "zl"))
    shot, pair = ("y", "x", "c"), ("yh", "zh", "zl")
    return jax.shard_map(
        shards,
        mesh=fine,
        in_specs=(P(None, shot, None, pair), P(shot)),
        out_specs=P(None, shot, pair, None),
        check_vma=False,
    )
```
